32 devices in a mesh: band: 8 (over y, x, core), field: 4 (over z).
Axes of the slice: x: 2, y: 2, z: 4, core: 2. Of those that a mesh axis runs over, the one named last changes fastest.
Arguments:
- fourier: bfloat16 [144, 256, 2, 1024], P('field', 'band'), may hold values from -6 to 6
- row_length: int32 [256], P('band'), may hold values from 20 to 2064, as said below
- wave_order: int32 [512], replicated, may hold values from 0 to 511, each once
- legendre: bfloat16 [512, 1025, 128], P(('band', 'field')), may hold values from -0.375 to 0.375
- vertical: bfloat16 [2, 72, 72], replicated, may hold values from -0.75 to 0.75
Outputs:
- returned: bfloat16 [144, 256, 2, 1024], P('field', 'band')
The draws below stay inside these ranges and needn't reach their ends.
Inputs may be any that keep to these rules, and one draw needn't show every extreme that they name: row_length[lat] is a multiple of 4 lying 0 to 12 above 20 + 16 * d with d = min(lat, 255 - lat); the two polar rows have length 20 and the two rows beside the equator lie 12 above. `wave_order`: each pair index appears once.
All inputs are finite; a program needn't handle non-finite values.
Results may differ from the reference program's by a relative error of at most 0.0049.
Values may be sent and summed in bfloat16 or wider, within the bound.
A program may use at most 128 MiB of HBM per device.

```python
import jax
import jax.numpy as jnp
from jax import lax

MW = 1024
LEV = 72
NLAT = 256
NLATH = 128
FL = 144
NPAIR = 512
ROW_STEP = 16


def draw_row_length(key, part):
    lat_ids = jnp.arange(NLAT, dtype=jnp.int32)
    from_pole = jnp.minimum(lat_ids, NLAT - 1 - lat_ids)
    jitter = jax.random.randint(key, (NLAT,), 0, 4, dtype=jnp.int32)
    jitter = jnp.where(from_pole == 0, 0, jitter)
    jitter = jnp.where(from_pole == NLAT // 2 - 1, 3, jitter)
    return (20 + ROW_STEP * from_pole + 4 * jitter).astype(jnp.int32)


def steps_of(stream_key, extent, split, low, top_value):
    gain, own = 1.0, jax.random.fold_in(stream_key, 6)
    for dim, blocks in split:
        heights = jnp.exp(jax.random.uniform(jax.random.fold_in(own, dim), (blocks,), jnp.float32, low / len(split), top_value / len(split)))
        gain = gain * jnp.repeat(heights, extent[dim] // blocks).reshape([-1 if axis == dim else 1 for axis in range(len(extent))])
    return gain


def bell_draw(stream_key, dims, deviation, limit, cuts=(), kind=jnp.bfloat16):
    level = steps_of(stream_key, dims, cuts, -0.22, 0.18) if cuts else 1.0
    result = jax.random.normal(stream_key, dims, jnp.float32) * deviation * level
    return jnp.minimum(jnp.maximum(result, -limit), limit).astype(kind)


def setup_inputs(seed: int = 0) -> dict:
    splits = jax.random.split(jax.random.key(seed), 6)
    fourier = bell_draw(splits[0], (FL, NLAT, 2, MW), 1.0, 6.0, ((0, 4), (1, 8)))
    row_length = draw_row_length(jax.random.fold_in(splits[5], 71), 0)
    wave_order = jax.random.permutation(splits[2], NPAIR).astype(jnp.int32)
    legendre = bell_draw(splits[3], (NPAIR, MW + 1, NLATH), NLAT ** -0.5, 0.375, ((0, 32),))
    vertical = bell_draw(splits[4], (2, LEV, LEV), LEV ** -0.5, 0.75)
    return {"fourier": fourier, "row_length": row_length, "wave_order": wave_order, "legendre": legendre, "vertical": vertical}


def pair_table(table_pair, first_wave):
    row_ids = jnp.arange(MW + 1, dtype=jnp.int32)
    boundary = MW - first_wave
    degree = jnp.where(row_ids < boundary, row_ids, row_ids - boundary)
    parity = (1 - 2 * (degree % 2)).astype(jnp.float32)
    northern = table_pair.astype(jnp.float32)
    southern = jnp.flip(northern, axis=1) * parity[:, None]
    owner_mask = jnp.stack([row_ids < boundary, row_ids >= boundary])
    return jnp.concatenate([northern, southern], axis=1), owner_mask


def reference(fourier, row_length, wave_order, legendre, vertical):
    wave_ids = jnp.arange(MW, dtype=jnp.int32)
    wave_count = jnp.minimum(MW, row_length // 2)
    in_range = wave_ids[None, :] < wave_count[:, None]
    masked = jnp.where(in_range[None, :, None, :], fourier, jnp.zeros((), fourier.dtype))
    ordering = jnp.stack([wave_order, MW - 1 - wave_order], axis=1).reshape(MW)
    paired = jnp.take(masked, ordering, axis=3).reshape(FL, NLAT, 2, NPAIR, 2).transpose(3, 4, 0, 2, 1)
    mixing = vertical.astype(jnp.float32)
    highest = lax.Precision.HIGHEST

    def transform_pair(inputs):
        values, table_pair, first_wave = inputs
        full_table, owner_mask = pair_table(table_pair, first_wave)
        flat_values = values.reshape(2, FL * 2, NLAT).astype(jnp.float32)
        spectral = jnp.einsum("scl,rl->scr", flat_values, full_table, precision=highest)
        spectral = jnp.where(owner_mask[:, None, :], spectral, 0.0).astype(jnp.bfloat16)
        shaped = spectral.reshape(2, 2, LEV, 2, MW + 1).astype(jnp.float32)
        updated = jnp.einsum("qab,sqbcr->sqacr", mixing, shaped, precision=highest).astype(jnp.bfloat16)
        updated_flat = updated.reshape(2, FL * 2, MW + 1).astype(jnp.float32)
        grid_part = jnp.einsum("scr,rl->scl", updated_flat, full_table, precision=highest)
        return grid_part.astype(jnp.bfloat16).reshape(2, FL, 2, NLAT)

    pieces = lax.map(transform_pair, (paired, legendre, wave_order))
    sorted_back = pieces.transpose(2, 4, 3, 0, 1).reshape(FL, NLAT, 2, MW)
    position = jnp.zeros((MW,), jnp.int32).at[ordering].set(wave_ids)
    restored = jnp.take(sorted_back, position, axis=3)
    return jnp.where(in_range[None, :, None, :], restored, jnp.zeros((), restored.dtype))
```

```python
import functools

import jax
import jax.numpy as jnp
from jax import lax
from jax.experimental import pallas as pl
from jax.experimental.pallas import tpu as pltpu
from jax.sharding import PartitionSpec as P

MESH = pl.DeviceIdType.MESH


def exchange_kernel(bands, fields, src, dst, send_sem, recv_sem, own_sem):
    total = bands * fields
    band, field = lax.axis_index("band"), lax.axis_index("field")
    me = band * fields + field

    def other(step):
        peer = lax.rem(me + step, total)
        return peer, (peer // fields, lax.rem(peer, fields))

    barrier = pltpu.get_barrier_semaphore()

    @pl.loop(1, total)
    def _(step):
        _, where = other(step)
        pl.semaphore_signal(barrier, inc=1, device_id=where, device_id_type=MESH)

    own = pltpu.make_async_copy(src.at[me], dst.at[me], own_sem)
    own.start()
    pl.semaphore_wait(barrier, total - 1)

    def copy(step):
        peer, where = other(step)
        return pltpu.make_async_remote_copy(
            src_ref=src.at[peer],
            dst_ref=dst.at[me],
            send_sem=send_sem.at[step],
            recv_sem=recv_sem.at[step],
            device_id=where,
            device_id_type=MESH,
        )

    @pl.loop(1, total)
    def _(step):
        copy(step).start()

    @pl.loop(1, total)
    def _(step):
        copy(step).wait_send()
        peer = lax.rem(me + total - step, total)
        pltpu.make_async_remote_copy(
            src_ref=src.at[peer],
            dst_ref=dst.at[peer],
            send_sem=send_sem.at[step],
            recv_sem=recv_sem.at[step],
            device_id=(peer // fields, lax.rem(peer, fields)),
            device_id_type=MESH,
        ).wait_recv()

    own.wait()


def exchange(data, bands, fields, ident):
    total = bands * fields
    return pl.pallas_call(
        functools.partial(exchange_kernel, bands, fields),
        out_shape=jax.ShapeDtypeStruct(data.shape, data.dtype),
        in_specs=[pl.BlockSpec(memory_space=pl.ANY)],
        out_specs=pl.BlockSpec(memory_space=pl.ANY),
        scratch_shapes=[
            pltpu.SemaphoreType.DMA((total,)),
            pltpu.SemaphoreType.DMA((total,)),
            pltpu.SemaphoreType.DMA,
        ],
        compiler_params=pltpu.CompilerParams(collective_id=ident, has_side_effects=True),
    )(data)


def pair_kernel(waves, first, x_ref, table_ref, mix_ref, out_ref):
    table = table_ref[0]
    rows, half = table.shape
    boundary = waves - first[pl.program_id(0)]
    up = lax.broadcasted_iota(jnp.int32, (half, half), 0)
    across = lax.broadcasted_iota(jnp.int32, (half, half), 1)
    turn = (up + across == half - 1).astype(jnp.float32).astype(jnp.bfloat16)
    southern = jnp.dot(table, turn, preferred_element_type=jnp.float32)
    northern = table.astype(jnp.float32)
    row_ids = lax.broadcasted_iota(jnp.int32, (rows, half), 0)
    held = row_ids < boundary
    degree = jnp.where(held, row_ids, row_ids - boundary)
    southern = jnp.where(degree % 2 == 0, southern, -southern)
    zero = jnp.zeros((), jnp.float32)
    full = jnp.concatenate(
        [
            jnp.where(held, northern, zero).astype(jnp.bfloat16),
            jnp.where(held, southern, zero).astype(jnp.bfloat16),
            jnp.where(held, zero, northern).astype(jnp.bfloat16),
            jnp.where(held, zero, southern).astype(jnp.bfloat16),
        ],
        axis=1,
    )
    spectral = lax.dot_general(
        x_ref[0], full, (((1,), (1,)), ((), ())), preferred_element_type=jnp.float32
    ).astype(jnp.bfloat16)
    updated = jnp.dot(mix_ref[...], spectral, preferred_element_type=jnp.float32).astype(jnp.bfloat16)
    out_ref[0] = jnp.dot(updated, full, preferred_element_type=jnp.float32).astype(jnp.bfloat16)


def transform(values, legendre, mixing, pair_first, waves):
    pairs, columns, span = values.shape
    rows, half = legendre.shape[1:]
    flops = 2 * pairs * columns * rows * (2 * span + columns)
    return pl.pallas_call(
        functools.partial(pair_kernel, waves),
        grid_spec=pltpu.PrefetchScalarGridSpec(
            num_scalar_prefetch=1,
            grid=(pairs,),
            in_specs=[
                pl.BlockSpec((1, columns, span), lambda k, first: (k, 0, 0)),
                pl.BlockSpec((1, rows, half), lambda k, first: (k, 0, 0)),
                pl.BlockSpec((columns, columns), lambda k, first: (0, 0)),
            ],
            out_specs=pl.BlockSpec((1, columns, span), lambda k, first: (k, 0, 0)),
        ),
        out_shape=jax.ShapeDtypeStruct(values.shape, jnp.bfloat16),
        compiler_params=pltpu.CompilerParams(vmem_limit_bytes=48 * 1024 * 1024),
        cost_estimate=pl.CostEstimate(
            flops=flops, bytes_accessed=4 * values.size + 2 * legendre.size, transcendentals=0
        ),
    )(pair_first, values, legendre, mixing)


def mixing_matrix(vertical, fields):
    levels = vertical.shape[1]
    total = 2 * levels
    blocks = jnp.zeros((2, levels, 2, levels), vertical.dtype)
    blocks = blocks.at[0, :, 0, :].set(vertical[0]).at[1, :, 1, :].set(vertical[1])
    block = blocks.reshape(fields, total // fields, fields, total // fields)
    parts = jnp.eye(2, dtype=vertical.dtype)
    return jnp.einsum("zfyg,cd->zcfydg", block, parts).reshape(2 * total, 2 * total)


def per_device(fourier, row_length, wave_order, legendre, vertical):
    levels, lats, _, waves = fourier.shape
    bands, fields = lax.axis_size("band"), lax.axis_size("field")
    total = bands * fields
    pairs = legendre.shape[0]
    wave_ids = lax.iota(jnp.int32, waves)
    wave_count = jnp.minimum(waves, row_length // 2)
    in_range = wave_ids[None, :] < wave_count[:, None]
    nothing = jnp.zeros((), jnp.bfloat16)
    masked = jnp.where(in_range[None, :, None, :], fourier, nothing)
    ordering = jnp.stack([wave_order, waves - 1 - wave_order], axis=1).reshape(waves)
    choose = (ordering[:, None] == wave_ids[None, :]).astype(jnp.bfloat16)
    start_pair = (lax.axis_index("band") * fields + lax.axis_index("field")) * pairs
    pair_first = lax.dynamic_slice_in_dim(wave_order, start_pair, pairs)

    flat = masked.transpose(2, 0, 1, 3).reshape(2 * levels * lats, waves)
    outgoing = lax.dot_general(
        choose, flat, (((1,), (1,)), ((), ())), preferred_element_type=jnp.float32
    ).astype(jnp.bfloat16)
    arrived = exchange(outgoing.reshape(total, 2 * pairs, 2 * levels * lats), bands, fields, 0)
    values = arrived.reshape(bands, fields, pairs, 2, 2 * levels, lats).transpose(2, 1, 4, 3, 0, 5)
    values = values.reshape(pairs, fields * 2 * levels, 2 * bands * lats)
    grid_part = transform(values, legendre, mixing_matrix(vertical, fields), pair_first, waves)
    back = grid_part.reshape(pairs, fields, 2 * levels, 2, bands, lats).transpose(4, 1, 0, 3, 2, 5)
    home = exchange(back.reshape(total, 2 * pairs, 2 * levels * lats), bands, fields, 1)
    restored = lax.dot_general(
        home.reshape(waves, 2 * levels * lats), choose, (((0,), (0,)), ((), ())),
        preferred_element_type=jnp.float32,
    ).astype(jnp.bfloat16)
    restored = restored.reshape(2, levels, lats, waves).transpose(1, 2, 0, 3)
    return jnp.where(in_range[None, :, None, :], restored, nothing)


def solution(mesh):
    placed = (P("field", "band", None, None), P("band"), P(), P(("band", "field"), None, None), P())
    return jax.shard_map(
        per_device,
        mesh=mesh,
        in_specs=placed,
        out_specs=P("field", "band", None, None),
        check_vma=False,
    )
```

```python
import functools

import jax
import jax.numpy as jnp
from jax import lax
from jax.experimental import pallas as pl
from jax.experimental.pallas import tpu as pltpu
from jax.sharding import PartitionSpec as P

MESH = pl.DeviceIdType.MESH


def exchange_kernel(bands, fields, src, dst, send_sem, recv_sem, own_sem):
    total = bands * fields
    band, field = lax.axis_index("band"), lax.axis_index("field")
    me = band * fields + field

    def other(step):
        peer = lax.rem(me + step, total)
        return peer, (peer // fields, lax.rem(peer, fields))

    barrier = pltpu.get_barrier_semaphore()

    @pl.loop(1, total)
    def _(step):
        _, where = other(step)
        pl.semaphore_signal(barrier, inc=1, device_id=where, device_id_type=MESH)

    own = pltpu.make_async_copy(src.at[me], dst.at[me], own_sem)
    own.start()
    pl.semaphore_wait(barrier, total - 1)

    def copy(step):
        peer, where = other(step)
        return pltpu.make_async_remote_copy(
            src_ref=src.at[peer],
            dst_ref=dst.at[me],
            send_sem=send_sem.at[step],
            recv_sem=recv_sem.at[step],
            device_id=where,
            device_id_type=MESH,
        )

    @pl.loop(1, total)
    def _(step):
        copy(step).start()

    @pl.loop(1, total)
    def _(step):
        copy(step).wait_send()
        peer = lax.rem(me + total - step, total)
        pltpu.make_async_remote_copy(
            src_ref=src.at[peer],
            dst_ref=dst.at[peer],
            send_sem=send_sem.at[step],
            recv_sem=recv_sem.at[step],
            device_id=(peer // fields, lax.rem(peer, fields)),
            device_id_type=MESH,
        ).wait_recv()

    own.wait()


def exchange(data, bands, fields, ident):
    total = bands * fields
    return pl.pallas_call(
        functools.partial(exchange_kernel, bands, fields),
        out_shape=jax.ShapeDtypeStruct(data.shape, data.dtype),
        in_specs=[pl.BlockSpec(memory_space=pl.ANY)],
        out_specs=pl.BlockSpec(memory_space=pl.ANY),
        scratch_shapes=[
            pltpu.SemaphoreType.DMA((total,)),
            pltpu.SemaphoreType.DMA((total,)),
            pltpu.SemaphoreType.DMA,
        ],
        compiler_params=pltpu.CompilerParams(collective_id=ident, has_side_effects=True),
    )(data)


def pair_kernel(waves, first, x_ref, table_ref, mix_ref, out_ref):
    full = masked_table(waves, first[pl.program_id(0)], table_ref[0])
    out_ref[0] = there_and_back(x_ref[0], full, mix_ref[...]).astype(jnp.bfloat16)


def transform(values, legendre, mixing, pair_first, waves):
    pairs, columns, span = values.shape
    rows, half = legendre.shape[1:]
    flops = 2 * pairs * columns * rows * (2 * span + columns)
    return pl.pallas_call(
        functools.partial(pair_kernel, waves),
        grid_spec=pltpu.PrefetchScalarGridSpec(
            num_scalar_prefetch=1,
            grid=(pairs,),
            in_specs=[
                pl.BlockSpec((1, columns, span), lambda k, first: (k, 0, 0)),
                pl.BlockSpec((1, rows, half), lambda k, first: (k, 0, 0)),
                pl.BlockSpec((columns, columns), lambda k, first: (0, 0)),
            ],
            out_specs=pl.BlockSpec((1, columns, span), lambda k, first: (k, 0, 0)),
        ),
        out_shape=jax.ShapeDtypeStruct(values.shape, jnp.bfloat16),
        compiler_params=pltpu.CompilerParams(vmem_limit_bytes=48 * 1024 * 1024),
        cost_estimate=pl.CostEstimate(
            flops=flops, bytes_accessed=4 * values.size + 2 * legendre.size, transcendentals=0
        ),
    )(pair_first, values, legendre, mixing)


def swap_groups(parts, lats):
    lane_group = lax.broadcasted_iota(jnp.int32, parts[0].shape, 1) // lats
    swapped = []
    for j in range(len(parts)):
        merged = None
        for i, part in enumerate(parts):
            shift = ((i - j) * lats) % 128
            turned = pltpu.roll(part, shift, 1) if shift else part
            merged = turned if merged is None else jnp.where(lane_group == i, turned, merged)
        swapped.append(merged)
    return swapped


def masked_table(waves, first_wave, table):
    rows, half = table.shape
    boundary = waves - first_wave
    up = lax.broadcasted_iota(jnp.int32, (half, half), 0)
    across = lax.broadcasted_iota(jnp.int32, (half, half), 1)
    turn = (up + across == half - 1).astype(jnp.float32).astype(jnp.bfloat16)
    southern = jnp.dot(table, turn, preferred_element_type=jnp.float32)
    northern = table.astype(jnp.float32)
    row_ids = lax.broadcasted_iota(jnp.int32, (rows, half), 0)
    held = row_ids < boundary
    degree = jnp.where(held, row_ids, row_ids - boundary)
    southern = jnp.where(degree % 2 == 0, southern, -southern)
    zero = jnp.zeros((), jnp.float32)
    return jnp.concatenate(
        [
            jnp.where(held, northern, zero).astype(jnp.bfloat16),
            jnp.where(held, southern, zero).astype(jnp.bfloat16),
            jnp.where(held, zero, northern).astype(jnp.bfloat16),
            jnp.where(held, zero, southern).astype(jnp.bfloat16),
        ],
        axis=1,
    )


def there_and_back(values, full, mixing):
    spectral = lax.dot_general(
        values, full, (((1,), (1,)), ((), ())), preferred_element_type=jnp.float32
    ).astype(jnp.bfloat16)
    updated = jnp.dot(mixing, spectral, preferred_element_type=jnp.float32).astype(jnp.bfloat16)
    return jnp.dot(updated, full, preferred_element_type=jnp.float32)


def packed_kernel(waves, bands, fields, lats, first, x_ref, table_ref, mix_ref, out_ref, held_ref):
    k = pl.program_id(0)
    count, tiles = x_ref.shape[1], x_ref.shape[2] // 128
    group = 128 // lats
    rows = fields * tiles

    @pl.when(k == 0)
    def _():
        @pl.loop(0, bands)
        def _(band):
            for field in range(fields):
                for tile in range(tiles):
                    at = (field * tiles + tile) * count
                    held_ref[band, at : at + count, :] = x_ref[
                        band * fields + field, :, tile * 128 : (tile + 1) * 128
                    ].astype(jnp.float32)

    def place(slot):
        return pl.ds(2 * k + slot, rows, stride=count)

    gathered = [[] for _ in range(group)]
    for slot in range(2):
        for start in range(0, bands, group):
            parts = [held_ref[start + i, place(slot), :] for i in range(group)]
            for j, part in enumerate(swap_groups(parts, lats)):
                gathered[j].append(part)
    values = jnp.concatenate([jnp.concatenate(g, axis=1) for g in gathered], axis=0).astype(jnp.bfloat16)
    full = masked_table(waves, first[k], table_ref[0])
    result = there_and_back(values, full, mix_ref[...])
    for slot in range(2):
        for start in range(0, bands, group):
            at = (slot * bands + start) * lats
            parts = [result[j * rows : (j + 1) * rows, at : at + 128] for j in range(group)]
            for i, part in enumerate(swap_groups(parts, lats)):
                held_ref[start + i, place(slot), :] = part

    @pl.when(k == pl.num_programs(0) - 1)
    def _():
        @pl.loop(0, bands)
        def _(band):
            for field in range(fields):
                for tile in range(tiles):
                    at = (field * tiles + tile) * count
                    out_ref[band * fields + field, :, tile * 128 : (tile + 1) * 128] = held_ref[
                        band, at : at + count, :
                    ].astype(jnp.bfloat16)


def packed_transform(arrived, legendre, mixing, pair_first, waves, bands, fields, lats):
    total, count, width = arrived.shape
    pairs, rows, half = legendre.shape
    columns = mixing.shape[0]
    flops = 2 * pairs * columns * rows * (4 * bands * lats + columns)
    whole = pl.BlockSpec((total, count, width), lambda k, first: (0, 0, 0))
    return pl.pallas_call(
        functools.partial(packed_kernel, waves, bands, fields, lats),
        grid_spec=pltpu.PrefetchScalarGridSpec(
            num_scalar_prefetch=1,
            grid=(pairs,),
            in_specs=[
                whole,
                pl.BlockSpec((1, rows, half), lambda k, first: (k, 0, 0)),
                pl.BlockSpec((columns, columns), lambda k, first: (0, 0)),
            ],
            out_specs=whole,
            scratch_shapes=[pltpu.VMEM((bands, fields * width // 128 * count, 128), jnp.float32)],
        ),
        out_shape=jax.ShapeDtypeStruct(arrived.shape, jnp.bfloat16),
        compiler_params=pltpu.CompilerParams(vmem_limit_bytes=52 * 1024 * 1024),
        cost_estimate=pl.CostEstimate(
            flops=flops, bytes_accessed=4 * arrived.size + 2 * legendre.size, transcendentals=0
        ),
    )(pair_first, arrived, legendre, mixing)


def mixing_matrix(vertical, fields, group):
    levels = vertical.shape[1]
    total = 2 * levels
    blocks = jnp.zeros((2, levels, 2, levels), vertical.dtype)
    blocks = blocks.at[0, :, 0, :].set(vertical[0]).at[1, :, 1, :].set(vertical[1])
    block = blocks.reshape(fields, total // fields, fields, total // fields)
    parts = jnp.eye(2, dtype=vertical.dtype)
    matrix = jnp.einsum("zfyg,cd->zcfydg", block, parts)
    if group > 1:
        tiles = 2 * total // fields // group
        matrix = matrix.reshape(fields, tiles, group, fields, tiles, group).transpose(2, 0, 1, 5, 3, 4)
    return matrix.reshape(2 * total, 2 * total)


def per_device(fourier, row_length, wave_order, legendre, vertical):
    levels, lats, _, waves = fourier.shape
    bands, fields = lax.axis_size("band"), lax.axis_size("field")
    total = bands * fields
    pairs = legendre.shape[0]
    wave_ids = lax.iota(jnp.int32, waves)
    wave_count = jnp.minimum(waves, row_length // 2)
    in_range = wave_ids[None, :] < wave_count[:, None]
    nothing = jnp.zeros((), jnp.bfloat16)
    masked = jnp.where(in_range[None, :, None, :], fourier, nothing)
    ordering = jnp.stack([wave_order, waves - 1 - wave_order], axis=1).reshape(waves)
    choose = (ordering[:, None] == wave_ids[None, :]).astype(jnp.bfloat16)
    start_pair = (lax.axis_index("band") * fields + lax.axis_index("field")) * pairs
    pair_first = lax.dynamic_slice_in_dim(wave_order, start_pair, pairs)

    flat = masked.transpose(2, 0, 1, 3).reshape(2 * levels * lats, waves)
    outgoing = lax.dot_general(
        choose, flat, (((1,), (1,)), ((), ())), preferred_element_type=jnp.float32
    ).astype(jnp.bfloat16)
    arrived = exchange(outgoing.reshape(total, 2 * pairs, 2 * levels * lats), bands, fields, 0)
    group = 128 // lats
    fits = 128 % lats == 0 and bands % group == 0 and 2 * levels % group == 0
    if fits and (2 * levels // group * fields) % 8 == 0 and 2 * pairs % 16 == 0:
        mixing = mixing_matrix(vertical, fields, group)
        back = packed_transform(arrived, legendre, mixing, pair_first, waves, bands, fields, lats)
    else:
        values = arrived.reshape(bands, fields, pairs, 2, 2 * levels, lats).transpose(2, 1, 4, 3, 0, 5)
        values = values.reshape(pairs, fields * 2 * levels, 2 * bands * lats)
        grid_part = transform(values, legendre, mixing_matrix(vertical, fields, 1), pair_first, waves)
        back = grid_part.reshape(pairs, fields, 2 * levels, 2, bands, lats).transpose(4, 1, 0, 3, 2, 5)
        back = back.reshape(total, 2 * pairs, 2 * levels * lats)
    home = exchange(back, bands, fields, 1)
    restored = lax.dot_general(
        home.reshape(waves, 2 * levels * lats), choose, (((0,), (0,)), ((), ())),
        preferred_element_type=jnp.float32,
    ).astype(jnp.bfloat16)
    restored = restored.reshape(2, levels, lats, waves).transpose(1, 2, 0, 3)
    return jnp.where(in_range[None, :, None, :], restored, nothing)


def solution(mesh):
    placed = (P("field", "band", None, None), P("band"), P(), P(("band", "field"), None, None), P())
    return jax.shard_map(
        per_device,
        mesh=mesh,
        in_specs=placed,
        out_specs=P("field", "band", None, None),
        check_vma=False,
    )
```

```python
import functools

import jax
import jax.numpy as jnp
import numpy as np
from jax import lax
from jax.experimental import pallas as pl
from jax.experimental.pallas import tpu as pltpu
from jax.sharding import PartitionSpec as P

MESH = pl.DeviceIdType.MESH


def exchange_kernel(bands, fields, src, dst, send_sem, recv_sem, own_sem):
    total = bands * fields
    band, field = lax.axis_index("band"), lax.axis_index("field")
    me = band * fields + field

    def other(step):
        peer = lax.rem(me + step, total)
        return peer, (peer // fields, lax.rem(peer, fields))

    barrier = pltpu.get_barrier_semaphore()

    @pl.loop(1, total)
    def _(step):
        _, where = other(step)
        pl.semaphore_signal(barrier, inc=1, device_id=where, device_id_type=MESH)

    own = pltpu.make_async_copy(src.at[me], dst.at[me], own_sem)
    own.start()
    pl.semaphore_wait(barrier, total - 1)

    def copy(step):
        peer, where = other(step)
        return pltpu.make_async_remote_copy(
            src_ref=src.at[peer],
            dst_ref=dst.at[me],
            send_sem=send_sem.at[step],
            recv_sem=recv_sem.at[step],
            device_id=where,
            device_id_type=MESH,
        )

    @pl.loop(1, total)
    def _(step):
        copy(step).start()

    @pl.loop(1, total)
    def _(step):
        copy(step).wait_send()
        peer = lax.rem(me + total - step, total)
        pltpu.make_async_remote_copy(
            src_ref=src.at[peer],
            dst_ref=dst.at[peer],
            send_sem=send_sem.at[step],
            recv_sem=recv_sem.at[step],
            device_id=(peer // fields, lax.rem(peer, fields)),
            device_id_type=MESH,
        ).wait_recv()

    own.wait()


def exchange(data, bands, fields, ident):
    total = bands * fields
    return pl.pallas_call(
        functools.partial(exchange_kernel, bands, fields),
        out_shape=jax.ShapeDtypeStruct(data.shape, data.dtype),
        in_specs=[pl.BlockSpec(memory_space=pl.ANY)],
        out_specs=pl.BlockSpec(memory_space=pl.ANY),
        scratch_shapes=[
            pltpu.SemaphoreType.DMA((total,)),
            pltpu.SemaphoreType.DMA((total,)),
            pltpu.SemaphoreType.DMA,
        ],
        compiler_params=pltpu.CompilerParams(collective_id=ident, has_side_effects=True),
    )(data)


def pair_kernel(waves, first, x_ref, table_ref, mix_ref, out_ref):
    full = masked_table(waves, first[pl.program_id(0)], table_ref[0])
    out_ref[0] = there_and_back(x_ref[0], full, mix_ref[...]).astype(jnp.bfloat16)


def transform(values, legendre, mixing, pair_first, waves):
    pairs, columns, span = values.shape
    rows, half = legendre.shape[1:]
    flops = 2 * pairs * columns * rows * (2 * span + columns)
    return pl.pallas_call(
        functools.partial(pair_kernel, waves),
        grid_spec=pltpu.PrefetchScalarGridSpec(
            num_scalar_prefetch=1,
            grid=(pairs,),
            in_specs=[
                pl.BlockSpec((1, columns, span), lambda k, first: (k, 0, 0)),
                pl.BlockSpec((1, rows, half), lambda k, first: (k, 0, 0)),
                pl.BlockSpec((columns, columns), lambda k, first: (0, 0)),
            ],
            out_specs=pl.BlockSpec((1, columns, span), lambda k, first: (k, 0, 0)),
        ),
        out_shape=jax.ShapeDtypeStruct(values.shape, jnp.bfloat16),
        compiler_params=pltpu.CompilerParams(vmem_limit_bytes=48 * 1024 * 1024),
        cost_estimate=pl.CostEstimate(
            flops=flops, bytes_accessed=4 * values.size + 2 * legendre.size, transcendentals=0
        ),
    )(pair_first, values, legendre, mixing)


def swap_groups(parts, lats):
    lane_group = lax.broadcasted_iota(jnp.int32, parts[0].shape, 1) // lats
    swapped = []
    for j in range(len(parts)):
        merged = None
        for i, part in enumerate(parts):
            shift = ((i - j) * lats) % 128
            turned = pltpu.roll(part, shift, 1) if shift else part
            merged = turned if merged is None else jnp.where(lane_group == i, turned, merged)
        swapped.append(merged)
    return swapped


def masked_table(waves, first_wave, table):
    rows, half = table.shape
    boundary = waves - first_wave
    up = lax.broadcasted_iota(jnp.int32, (half, half), 0)
    across = lax.broadcasted_iota(jnp.int32, (half, half), 1)
    turn = (up + across == half - 1).astype(jnp.float32).astype(jnp.bfloat16)
    southern = jnp.dot(table, turn, preferred_element_type=jnp.float32)
    northern = table.astype(jnp.float32)
    row_ids = lax.broadcasted_iota(jnp.int32, (rows, half), 0)
    held = row_ids < boundary
    degree = jnp.where(held, row_ids, row_ids - boundary)
    southern = jnp.where(degree % 2 == 0, southern, -southern)
    zero = jnp.zeros((), jnp.float32)
    return jnp.concatenate(
        [
            jnp.where(held, northern, zero).astype(jnp.bfloat16),
            jnp.where(held, southern, zero).astype(jnp.bfloat16),
            jnp.where(held, zero, northern).astype(jnp.bfloat16),
            jnp.where(held, zero, southern).astype(jnp.bfloat16),
        ],
        axis=1,
    )


def there_and_back(values, full, mixing):
    spectral = lax.dot_general(
        values, full, (((1,), (1,)), ((), ())), preferred_element_type=jnp.float32
    ).astype(jnp.bfloat16)
    updated = jnp.dot(mixing, spectral, preferred_element_type=jnp.float32).astype(jnp.bfloat16)
    return jnp.dot(updated, full, preferred_element_type=jnp.float32)


ROUNDS = (2, 3, 1, 0)


def partner(field, turn):
    if turn == 0:
        return field
    if turn == 2:
        return lax.rem(field + 2, 4)
    return 3 - field if turn == 3 else field + 1 - 2 * lax.rem(field, 2)


def near_equator(band, bands):
    return (band >= bands // 4) & (band < bands - bands // 4)


def greet(band, field, bands):
    barrier = pltpu.get_barrier_semaphore()

    @pl.loop(1, bands)
    def _(step):
        where = (lax.rem(band + step, bands), field)
        pl.semaphore_signal(barrier, inc=1, device_id=where, device_id_type=MESH)

    for turn in (1, 2, 3):
        where = (band, partner(field, turn))
        pl.semaphore_signal(barrier, inc=1, device_id=where, device_id_type=MESH)
    pl.semaphore_wait(barrier, bands - 1 + 3)


def remote(src, dst, send, recv, where):
    return pltpu.make_async_remote_copy(
        src_ref=src, dst_ref=dst, send_sem=send, recv_sem=recv, device_id=where, device_id_type=MESH
    )


def outward_kernel(bands, src, dst, mid, plane_send, plane_recv, line_send, line_recv, own_sem):
    band, field = lax.axis_index("band"), lax.axis_index("field")
    low, high = bands // 4, bands - bands // 4
    middle = pl.ds(low, high - low)
    greet(band, field, bands)

    def landing(turn, slot, origin):
        return dst.at[field, slot, origin] if turn == 0 else mid.at[turn, slot, origin]

    def plane(turn, step, slot):
        peer = lax.rem(band + step, bands)
        return remote(
            src.at[peer, partner(field, turn), slot], landing(turn, slot, band),
            plane_send.at[turn, step, slot], plane_recv.at[turn, step, slot], (peer, field),
        )

    def arrival(turn, step, slot):
        peer = lax.rem(band + bands - step, bands)
        spot = landing(turn, slot, peer)
        return remote(
            spot, spot, plane_send.at[turn, step, slot], plane_recv.at[turn, step, slot], (peer, field)
        )

    def own(turn, slot):
        return pltpu.make_async_copy(
            src.at[band, partner(field, turn), slot], landing(turn, slot, band), own_sem.at[turn, slot]
        )

    def line(turn, slot):
        where = (band, partner(field, turn))
        if slot == 0:
            source, target = mid.at[turn, 0], dst.at[field, 0]
        else:
            source, target = mid.at[turn, 1, middle], dst.at[field, 1, middle]
        return remote(source, target, line_send.at[turn, slot], line_recv.at[turn, slot], where)

    def line_arrival(turn, slot):
        origin = partner(field, turn)
        spot = dst.at[origin, 0] if slot == 0 else dst.at[origin, 1, middle]
        return remote(
            spot, spot, line_send.at[turn, slot], line_recv.at[turn, slot], (band, origin)
        )

    for turn in ROUNDS:
        own(turn, 0).start()
        own(turn, 1).start()

        @pl.loop(1, bands)
        def _(step):
            plane(turn, step, 0).start()

            @pl.when(near_equator(band, bands))
            def _():
                plane(turn, step, 1).start()

    for turn in ROUNDS:
        own(turn, 0).wait()
        own(turn, 1).wait()

        @pl.loop(1, bands)
        def _(step):
            arrival(turn, step, 0).wait_recv()

            @pl.when(near_equator(lax.rem(band + bands - step, bands), bands))
            def _():
                arrival(turn, step, 1).wait_recv()

        if turn:
            line(turn, 0).start()
            line(turn, 1).start()

    for turn in ROUNDS:

        @pl.loop(1, bands)
        def _(step):
            plane(turn, step, 0).wait_send()

            @pl.when(near_equator(band, bands))
            def _():
                plane(turn, step, 1).wait_send()

        if turn:
            for slot in range(2):
                line(turn, slot).wait_send()
                line_arrival(turn, slot).wait_recv()


def homeward_kernel(
    bands, src, zeros, dst, mid, plane_send, plane_recv, line_send, line_recv, own_sem, zero_sem
):
    band, field = lax.axis_index("band"), lax.axis_index("field")
    low, high = bands // 4, bands - bands // 4
    middle = pl.ds(low, high - low)
    greet(band, field, bands)

    def held(turn, slot, target):
        return src.at[field, slot, target] if turn == 0 else mid.at[turn, slot, target]

    def plane(turn, step, slot):
        peer = lax.rem(band + step, bands)
        return remote(
            held(turn, slot, peer), dst.at[band, partner(field, turn), slot],
            plane_send.at[turn, step, slot], plane_recv.at[turn, step, slot], (peer, field),
        )

    def arrival(turn, step, slot):
        peer = lax.rem(band + bands - step, bands)
        spot = dst.at[peer, partner(field, turn), slot]
        return remote(
            spot, spot, plane_send.at[turn, step, slot], plane_recv.at[turn, step, slot], (peer, field)
        )

    def own(turn, slot):
        return pltpu.make_async_copy(
            held(turn, slot, band), dst.at[band, partner(field, turn), slot], own_sem.at[turn, slot]
        )

    def blank(peer, z):
        return pltpu.make_async_copy(zeros, dst.at[peer, z, 1], zero_sem.at[peer, z])

    def line(turn, slot):
        goal = partner(field, turn)
        if slot == 0:
            source, target = src.at[goal, 0], mid.at[turn, 0]
        else:
            source, target = src.at[goal, 1, middle], mid.at[turn, 1, middle]
        return remote(
            source, target, line_send.at[turn, slot], line_recv.at[turn, slot], (band, goal)
        )

    for turn in ROUNDS[:3]:
        line(turn, 0).start()
        line(turn, 1).start()

    for turn in (0,) + ROUNDS[:3]:
        if turn:
            line(turn, 0).wait_recv()
            line(turn, 1).wait_recv()

        @pl.loop(1, bands)
        def _(step):
            plane(turn, step, 0).start()

            @pl.when(near_equator(lax.rem(band + step, bands), bands))
            def _():
                plane(turn, step, 1).start()

        own(turn, 0).start()

        @pl.when(near_equator(band, bands))
        def _():
            own(turn, 1).start()

    @pl.when(jnp.logical_not(near_equator(band, bands)))
    def _():
        @pl.loop(0, bands)
        def _(peer):
            for z in range(4):
                blank(peer, z).start()

        @pl.loop(0, bands)
        def _(peer):
            for z in range(4):
                blank(peer, z).wait()

    for turn in (0,) + ROUNDS[:3]:
        own(turn, 0).wait()

        @pl.when(near_equator(band, bands))
        def _():
            own(turn, 1).wait()

        @pl.loop(1, bands)
        def _(step):
            plane(turn, step, 0).wait_send()
            arrival(turn, step, 0).wait_recv()

            @pl.when(near_equator(lax.rem(band + step, bands), bands))
            def _():
                plane(turn, step, 1).wait_send()

            @pl.when(near_equator(band, bands))
            def _():
                arrival(turn, step, 1).wait_recv()

        if turn:
            line(turn, 0).wait_send()
            line(turn, 1).wait_send()


def staged_scratch(bands, piece):
    return [
        pltpu.VMEM((4, 2, bands) + piece, jnp.bfloat16),
        pltpu.SemaphoreType.DMA((4, bands, 2)),
        pltpu.SemaphoreType.DMA((4, bands, 2)),
        pltpu.SemaphoreType.DMA((4, 2)),
        pltpu.SemaphoreType.DMA((4, 2)),
        pltpu.SemaphoreType.DMA((4, 2)),
    ]


def outward(data):
    bands, fields, _, count, width = data.shape
    return pl.pallas_call(
        functools.partial(outward_kernel, bands),
        out_shape=jax.ShapeDtypeStruct((fields, 2, bands, count, width), data.dtype),
        in_specs=[pl.BlockSpec(memory_space=pl.ANY)],
        out_specs=pl.BlockSpec(memory_space=pl.ANY),
        scratch_shapes=staged_scratch(bands, (count, width)),
        compiler_params=pltpu.CompilerParams(
            collective_id=0, has_side_effects=True, vmem_limit_bytes=12 * 1024 * 1024
        ),
    )(data)


def homeward(data):
    fields, _, bands, count, width = data.shape
    return pl.pallas_call(
        functools.partial(homeward_kernel, bands),
        out_shape=jax.ShapeDtypeStruct((bands, fields, 2, count, width), data.dtype),
        in_specs=[pl.BlockSpec(memory_space=pl.ANY)] * 2,
        out_specs=pl.BlockSpec(memory_space=pl.ANY),
        scratch_shapes=staged_scratch(bands, (count, width)) + [pltpu.SemaphoreType.DMA((bands, 4))],
        compiler_params=pltpu.CompilerParams(
            collective_id=1, has_side_effects=True, vmem_limit_bytes=12 * 1024 * 1024
        ),
    )(data, jnp.zeros((count, width), data.dtype))


def compact_table(waves, first_wave, table, spare, shared):
    rows, half = table.shape
    boundary = waves - first_wave
    row_ids = lax.broadcasted_iota(jnp.int32, (rows, half), 0)
    lanes = lax.broadcasted_iota(jnp.int32, (rows, half), 1)
    held = row_ids < boundary
    degree = jnp.where(held, row_ids, row_ids - boundary)
    even = degree % 2 == 0
    up = lax.broadcasted_iota(jnp.int32, (half, half), 0)
    across = lax.broadcasted_iota(jnp.int32, (half, half), 1)
    turn = (up + across == half - 1).astype(jnp.float32).astype(jnp.bfloat16)
    origin = jnp.where(across < half // 2, across + half // 2, half + half // 2 - 1 - across)
    halved = (up == origin).astype(jnp.float32).astype(jnp.bfloat16)
    northern = table.astype(jnp.float32)
    zero = jnp.zeros((), jnp.float32)
    second = jnp.where(held, zero, northern)
    moved = (lanes == spare) & (first_wave >= waves // 2 - 8)
    main = jnp.where(moved, second[:, shared : shared + 1], jnp.where(held, northern, zero))
    main = main.astype(jnp.bfloat16)
    southern = jnp.dot(main, turn, preferred_element_type=jnp.float32)
    southern = jnp.where(even, southern, -southern)
    extra = jnp.dot(second.astype(jnp.bfloat16), halved, preferred_element_type=jnp.float32)
    extra = jnp.where(even | (lanes < half // 2), extra, -extra)
    return jnp.concatenate([main, southern.astype(jnp.bfloat16), extra.astype(jnp.bfloat16)], axis=1)


def packed_kernel(waves, lats, spare, shared, first, x_ref, table_ref, mix_ref, out_ref, held_ref):
    k = pl.program_id(0)
    fields, _, bands, count, width = x_ref.shape
    tiles = width // 128
    group = 128 // lats
    rows = fields * tiles
    low, high = bands // 4, bands - bands // 4
    spans = [(0, 0, bands, 0), (1, low, high, bands)]

    @pl.when(k == 0)
    def _():
        for slot, begin, end, base in spans:

            @pl.loop(begin, end)
            def _(band):
                for field in range(fields):
                    for tile in range(tiles):
                        at = (field * tiles + tile) * count
                        held_ref[base - begin + band, at : at + count, :] = x_ref[
                            field, slot, band, :, tile * 128 : (tile + 1) * 128
                        ].astype(jnp.float32)

    place = pl.ds(k, rows, stride=count)
    slabs = bands + high - low
    gathered = [[] for _ in range(group)]
    for start in range(0, slabs, group):
        parts = [held_ref[start + i, place, :] for i in range(group)]
        for j, part in enumerate(swap_groups(parts, lats)):
            gathered[j].append(part)
    values = jnp.concatenate([jnp.concatenate(g, axis=1) for g in gathered], axis=0).astype(jnp.bfloat16)
    full = compact_table(waves, first[k], table_ref[0], spare, shared)
    result = there_and_back(values, full, mix_ref[...])
    for start in range(0, slabs, group):
        at = start * lats
        parts = [result[j * rows : (j + 1) * rows, at : at + 128] for j in range(group)]
        for i, part in enumerate(swap_groups(parts, lats)):
            held_ref[start + i, place, :] = part

    @pl.when(k == pl.num_programs(0) - 1)
    def _():
        for slot, begin, end, base in spans:

            @pl.loop(begin, end)
            def _(band):
                for field in range(fields):
                    for tile in range(tiles):
                        at = (field * tiles + tile) * count
                        out_ref[field, slot, band, :, tile * 128 : (tile + 1) * 128] = held_ref[
                            base - begin + band, at : at + count, :
                        ].astype(jnp.bfloat16)


def packed_transform(arrived, legendre, mixing, pair_first, waves, lats, spare, shared):
    fields, _, bands, count, width = arrived.shape
    pairs, rows, half = legendre.shape
    columns = mixing.shape[0]
    flops = 2 * pairs * columns * rows * (3 * bands * lats + columns)
    whole = pl.BlockSpec(arrived.shape, lambda k, first: (0, 0, 0, 0, 0))
    slabs = bands + bands - 2 * (bands // 4)
    return pl.pallas_call(
        functools.partial(packed_kernel, waves, lats, spare, shared),
        grid_spec=pltpu.PrefetchScalarGridSpec(
            num_scalar_prefetch=1,
            grid=(pairs,),
            in_specs=[
                whole,
                pl.BlockSpec((1, rows, half), lambda k, first: (k, 0, 0)),
                pl.BlockSpec((columns, columns), lambda k, first: (0, 0)),
            ],
            out_specs=whole,
            scratch_shapes=[pltpu.VMEM((slabs, fields * width // 128 * count, 128), jnp.float32)],
        ),
        out_shape=jax.ShapeDtypeStruct(arrived.shape, jnp.bfloat16),
        compiler_params=pltpu.CompilerParams(vmem_limit_bytes=52 * 1024 * 1024),
        cost_estimate=pl.CostEstimate(
            flops=flops, bytes_accessed=4 * arrived.size + 2 * legendre.size, transcendentals=0
        ),
    )(pair_first, arrived, legendre, mixing)


def mixing_by_rows(vertical, fields, group):
    levels = vertical.shape[1]
    per_field = 2 * levels // fields
    tiles = 2 * per_field // group
    j, z, t = np.meshgrid(np.arange(group), np.arange(fields), np.arange(tiles), indexing="ij")
    column = (t * group + j).reshape(-1)
    part = column // per_field
    level = z.reshape(-1) * per_field + column % per_field
    rows = level.size
    choose = np.zeros((2, rows, levels), np.float32)
    choose[level // levels, np.arange(rows), level % levels] = 1
    choose = jnp.asarray(choose, jnp.bfloat16)
    left = jnp.einsum("qra,qab->rqb", choose, vertical, preferred_element_type=jnp.float32)
    both = jnp.einsum(
        "rqb,qsb->rs", left.astype(jnp.bfloat16), choose, preferred_element_type=jnp.float32
    )
    return jnp.where(jnp.asarray(part[:, None] == part[None, :]), both, 0.0).astype(jnp.bfloat16)


def mixing_matrix(vertical, fields):
    levels = vertical.shape[1]
    total = 2 * levels
    blocks = jnp.zeros((2, levels, 2, levels), vertical.dtype)
    blocks = blocks.at[0, :, 0, :].set(vertical[0]).at[1, :, 1, :].set(vertical[1])
    block = blocks.reshape(fields, total // fields, fields, total // fields)
    parts = jnp.eye(2, dtype=vertical.dtype)
    return jnp.einsum("zfyg,cd->zcfydg", block, parts).reshape(2 * total, 2 * total)


def spread_waves(choose, masked):
    levels, lats, _, waves = masked.shape
    flat = masked.transpose(2, 0, 1, 3).reshape(2 * levels * lats, waves)
    return lax.dot_general(
        choose, flat, (((1,), (1,)), ((), ())), preferred_element_type=jnp.float32
    ).astype(jnp.bfloat16)


def gather_waves(home, choose, shape):
    levels, lats, _, waves = shape
    restored = lax.dot_general(
        home, choose, (((0,), (0,)), ((), ())), preferred_element_type=jnp.float32
    ).astype(jnp.bfloat16)
    return restored.reshape(2, levels, lats, waves).transpose(1, 2, 0, 3)


def per_device(fourier, row_length, wave_order, legendre, vertical):
    levels, lats, _, waves = fourier.shape
    bands, fields = lax.axis_size("band"), lax.axis_size("field")
    band = lax.axis_index("band")
    total = bands * fields
    pairs, _, half = legendre.shape
    wave_ids = lax.iota(jnp.int32, waves)
    wave_count = jnp.minimum(waves, row_length // 2)
    in_range = (wave_ids[None, :] < wave_count[:, None])[None, :, None, :]
    nothing = jnp.zeros((), jnp.bfloat16)
    masked = jnp.where(in_range, fourier, nothing)
    start_pair = (band * fields + lax.axis_index("field")) * pairs
    pair_first = lax.dynamic_slice_in_dim(wave_order, start_pair, pairs)
    width = 2 * levels * lats

    if (bands, fields, lats, half, waves, pairs, levels) == (8, 4, 32, 128, 1024, 16, 36):
        spare, shared, edge = half // 4, half // 2 - 1, waves // 2
        turned = band >= bands // 2
        in_band = (band == 1) | (band == bands - 2)
        spare_lat = jnp.where(turned, lats - 1, 0)
        shared_lat = jnp.where(turned, 0, lats - 1)
        lat_ids = lax.iota(jnp.int32, lats)[None, :, None, None]
        wave_at = wave_ids[None, None, None, :]
        to_spare = in_band & (lat_ids == spare_lat) & (wave_at >= edge - 8) & (wave_at < edge)
        to_shared = in_band & (lat_ids == shared_lat) & (wave_at >= edge) & (wave_at < edge + 8)
        row = lax.dynamic_slice_in_dim(fourier, shared_lat, 1, axis=1)[..., edge : edge + 8]
        count = lax.dynamic_slice_in_dim(wave_count, shared_lat, 1, axis=0)
        row = jnp.where(wave_ids[edge : edge + 8] < count[0], row, nothing)
        pad = ((0, 0), (0, 0), (0, 0), (edge - 8, waves - edge))
        masked = jnp.where(to_spare, jnp.pad(jnp.flip(row, 3), pad), masked)

        by_holder = wave_order.reshape(total, pairs)
        ordering = jnp.concatenate([by_holder, waves - 1 - by_holder], axis=1).reshape(waves)
        choose = (ordering[:, None] == wave_ids[None, :]).astype(jnp.bfloat16)
        outgoing = spread_waves(choose, masked).reshape(bands, fields, 2, pairs, width)
        mixing = mixing_by_rows(vertical, fields, 128 // lats)
        back = packed_transform(
            outward(outgoing), legendre, mixing, pair_first, waves, lats, spare, shared
        )
        restored = gather_waves(homeward(back).reshape(waves, width), choose, fourier.shape)
        row = lax.dynamic_slice_in_dim(restored, spare_lat, 1, axis=1)[..., edge - 8 : edge]
        pad = ((0, 0), (0, 0), (0, 0), (edge, waves - edge - 8))
        restored = jnp.where(to_shared, jnp.pad(jnp.flip(row, 3), pad), restored)
        return jnp.where(in_range, restored, nothing)

    ordering = jnp.stack([wave_order, waves - 1 - wave_order], axis=1).reshape(waves)
    choose = (ordering[:, None] == wave_ids[None, :]).astype(jnp.bfloat16)
    outgoing = spread_waves(choose, masked)
    arrived = exchange(outgoing.reshape(total, 2 * pairs, width), bands, fields, 2)
    values = arrived.reshape(bands, fields, pairs, 2, 2 * levels, lats).transpose(2, 1, 4, 3, 0, 5)
    values = values.reshape(pairs, fields * 2 * levels, 2 * bands * lats)
    grid_part = transform(values, legendre, mixing_matrix(vertical, fields), pair_first, waves)
    back = grid_part.reshape(pairs, fields, 2 * levels, 2, bands, lats).transpose(4, 1, 0, 3, 2, 5)
    home = exchange(back.reshape(total, 2 * pairs, width), bands, fields, 3)
    return jnp.where(in_range, gather_waves(home.reshape(waves, width), choose, fourier.shape), nothing)


def solution(mesh):
    placed = (P("field", "band", None, None), P("band"), P(), P(("band", "field"), None, None), P())
    return jax.shard_map(
        per_device,
        mesh=mesh,
        in_specs=placed,
        out_specs=P("field", "band", None, None),
        check_vma=False,
    )
```

```python
import functools

import jax
import jax.numpy as jnp
import numpy as np
from jax import lax
from jax.experimental import pallas as pl
from jax.experimental.pallas import tpu as pltpu
from jax.sharding import PartitionSpec as P

MESH = pl.DeviceIdType.MESH


def exchange_kernel(bands, fields, src, dst, send_sem, recv_sem, own_sem):
    total = bands * fields
    band, field = lax.axis_index("band"), lax.axis_index("field")
    me = band * fields + field

    def other(step):
        peer = lax.rem(me + step, total)
        return peer, (peer // fields, lax.rem(peer, fields))

    barrier = pltpu.get_barrier_semaphore()

    @pl.loop(1, total)
    def _(step):
        _, where = other(step)
        pl.semaphore_signal(barrier, inc=1, device_id=where, device_id_type=MESH)

    own = pltpu.make_async_copy(src.at[me], dst.at[me], own_sem)
    own.start()
    pl.semaphore_wait(barrier, total - 1)

    def copy(step):
        peer, where = other(step)
        return pltpu.make_async_remote_copy(
            src_ref=src.at[peer],
            dst_ref=dst.at[me],
            send_sem=send_sem.at[step],
            recv_sem=recv_sem.at[step],
            device_id=where,
            device_id_type=MESH,
        )

    @pl.loop(1, total)
    def _(step):
        copy(step).start()

    @pl.loop(1, total)
    def _(step):
        copy(step).wait_send()
        peer = lax.rem(me + total - step, total)
        pltpu.make_async_remote_copy(
            src_ref=src.at[peer],
            dst_ref=dst.at[peer],
            send_sem=send_sem.at[step],
            recv_sem=recv_sem.at[step],
            device_id=(peer // fields, lax.rem(peer, fields)),
            device_id_type=MESH,
        ).wait_recv()

    own.wait()


def exchange(data, bands, fields, ident):
    total = bands * fields
    return pl.pallas_call(
        functools.partial(exchange_kernel, bands, fields),
        out_shape=jax.ShapeDtypeStruct(data.shape, data.dtype),
        in_specs=[pl.BlockSpec(memory_space=pl.ANY)],
        out_specs=pl.BlockSpec(memory_space=pl.ANY),
        scratch_shapes=[
            pltpu.SemaphoreType.DMA((total,)),
            pltpu.SemaphoreType.DMA((total,)),
            pltpu.SemaphoreType.DMA,
        ],
        compiler_params=pltpu.CompilerParams(collective_id=ident, has_side_effects=True),
    )(data)


def pair_kernel(waves, first, x_ref, table_ref, mix_ref, out_ref):
    full = masked_table(waves, first[pl.program_id(0)], table_ref[0])
    out_ref[0] = there_and_back(x_ref[0], full, mix_ref[...]).astype(jnp.bfloat16)


def transform(values, legendre, mixing, pair_first, waves):
    pairs, columns, span = values.shape
    rows, half = legendre.shape[1:]
    flops = 2 * pairs * columns * rows * (2 * span + columns)
    return pl.pallas_call(
        functools.partial(pair_kernel, waves),
        grid_spec=pltpu.PrefetchScalarGridSpec(
            num_scalar_prefetch=1,
            grid=(pairs,),
            in_specs=[
                pl.BlockSpec((1, columns, span), lambda k, first: (k, 0, 0)),
                pl.BlockSpec((1, rows, half), lambda k, first: (k, 0, 0)),
                pl.BlockSpec((columns, columns), lambda k, first: (0, 0)),
            ],
            out_specs=pl.BlockSpec((1, columns, span), lambda k, first: (k, 0, 0)),
        ),
        out_shape=jax.ShapeDtypeStruct(values.shape, jnp.bfloat16),
        compiler_params=pltpu.CompilerParams(vmem_limit_bytes=48 * 1024 * 1024),
        cost_estimate=pl.CostEstimate(
            flops=flops, bytes_accessed=4 * values.size + 2 * legendre.size, transcendentals=0
        ),
    )(pair_first, values, legendre, mixing)


def swap_groups(parts, lats):
    lane_group = lax.broadcasted_iota(jnp.int32, parts[0].shape, 1) // lats
    swapped = []
    for j in range(len(parts)):
        merged = None
        for i, part in enumerate(parts):
            shift = ((i - j) * lats) % 128
            turned = pltpu.roll(part, shift, 1) if shift else part
            merged = turned if merged is None else jnp.where(lane_group == i, turned, merged)
        swapped.append(merged)
    return swapped


def masked_table(waves, first_wave, table):
    rows, half = table.shape
    boundary = waves - first_wave
    up = lax.broadcasted_iota(jnp.int32, (half, half), 0)
    across = lax.broadcasted_iota(jnp.int32, (half, half), 1)
    turn = (up + across == half - 1).astype(jnp.float32).astype(jnp.bfloat16)
    southern = jnp.dot(table, turn, preferred_element_type=jnp.float32)
    northern = table.astype(jnp.float32)
    row_ids = lax.broadcasted_iota(jnp.int32, (rows, half), 0)
    held = row_ids < boundary
    degree = jnp.where(held, row_ids, row_ids - boundary)
    southern = jnp.where(degree % 2 == 0, southern, -southern)
    zero = jnp.zeros((), jnp.float32)
    return jnp.concatenate(
        [
            jnp.where(held, northern, zero).astype(jnp.bfloat16),
            jnp.where(held, southern, zero).astype(jnp.bfloat16),
            jnp.where(held, zero, northern).astype(jnp.bfloat16),
            jnp.where(held, zero, southern).astype(jnp.bfloat16),
        ],
        axis=1,
    )


def there_and_back(values, full, mixing):
    spectral = lax.dot_general(
        values, full, (((1,), (1,)), ((), ())), preferred_element_type=jnp.float32
    ).astype(jnp.bfloat16)
    updated = jnp.dot(mixing, spectral, preferred_element_type=jnp.float32).astype(jnp.bfloat16)
    return jnp.dot(updated, full, preferred_element_type=jnp.float32)


ROUNDS = (2, 3, 1, 0)


def partner(field, turn):
    if turn == 0:
        return field
    if turn == 2:
        return lax.rem(field + 2, 4)
    return 3 - field if turn == 3 else field + 1 - 2 * lax.rem(field, 2)


def near_equator(band, bands):
    return (band >= bands // 4) & (band < bands - bands // 4)


def greet(band, field, bands):
    barrier = pltpu.get_barrier_semaphore()

    @pl.loop(1, bands)
    def _(step):
        where = (lax.rem(band + step, bands), field)
        pl.semaphore_signal(barrier, inc=1, device_id=where, device_id_type=MESH)

    for turn in (1, 2, 3):
        where = (band, partner(field, turn))
        pl.semaphore_signal(barrier, inc=1, device_id=where, device_id_type=MESH)
    pl.semaphore_wait(barrier, bands - 1 + 3)


def remote(src, dst, send, recv, where):
    return pltpu.make_async_remote_copy(
        src_ref=src, dst_ref=dst, send_sem=send, recv_sem=recv, device_id=where, device_id_type=MESH
    )


def outward_kernel(bands, src, dst, mid, plane_send, plane_recv, line_send, line_recv, own_sem, last_sem):
    band, field = lax.axis_index("band"), lax.axis_index("field")
    middle = pl.ds(bands // 2 - 1, 2)
    greet(band, field, bands)

    def plane(turn, step, slot):
        peer = lax.rem(band + step, bands)
        return remote(
            src.at[peer, partner(field, turn), slot], mid.at[turn, slot, band],
            plane_send.at[turn, step, slot], plane_recv.at[turn, step, slot], (peer, field),
        )

    def arrival(turn, step, slot):
        peer = lax.rem(band + bands - step, bands)
        spot = mid.at[turn, slot, peer]
        return remote(
            spot, spot, plane_send.at[turn, step, slot], plane_recv.at[turn, step, slot], (peer, field)
        )

    def own(turn, slot):
        return pltpu.make_async_copy(
            src.at[band, partner(field, turn), slot], mid.at[turn, slot, band], own_sem.at[turn, slot]
        )

    def ends(turn, slot, origin):
        if slot == 0:
            return mid.at[turn, 0], dst.at[origin, 0]
        return mid.at[turn, 1, middle], dst.at[origin, 1, middle]

    def line(turn, slot):
        source, target = ends(turn, slot, field)
        where = (band, partner(field, turn))
        return remote(source, target, line_send.at[turn, slot], line_recv.at[turn, slot], where)

    def line_arrival(turn, slot):
        origin = partner(field, turn)
        spot = ends(turn, slot, origin)[1]
        return remote(
            spot, spot, line_send.at[turn, slot], line_recv.at[turn, slot], (band, origin)
        )

    def last(slot):
        source, target = ends(0, slot, field)
        return pltpu.make_async_copy(source, target, last_sem.at[slot])

    def begin(turn):
        own(turn, 0).start()
        own(turn, 1).start()

        @pl.loop(1, bands)
        def _(step):
            plane(turn, step, 0).start()

            @pl.when(near_equator(band, bands))
            def _():
                plane(turn, step, 1).start()

    begin(ROUNDS[0])
    for at, turn in enumerate(ROUNDS):
        own(turn, 0).wait()
        own(turn, 1).wait()

        @pl.loop(1, bands)
        def _(step):
            arrival(turn, step, 0).wait_recv()

            @pl.when(near_equator(lax.rem(band + bands - step, bands), bands))
            def _():
                arrival(turn, step, 1).wait_recv()

        if at + 1 < len(ROUNDS):
            begin(ROUNDS[at + 1])
        for pole, mate in ((0, bands - bands // 4 - 1), (bands - 1, bands // 4)):
            mid[turn, 0, pole] = mid[turn, 0, pole] + mid[turn, 1, mate]
        for slot in range(2):
            if turn:
                line(turn, slot).start()
            else:
                last(slot).start()

    for turn in ROUNDS:

        @pl.loop(1, bands)
        def _(step):
            plane(turn, step, 0).wait_send()

            @pl.when(near_equator(band, bands))
            def _():
                plane(turn, step, 1).wait_send()

        for slot in range(2):
            if turn:
                line(turn, slot).wait_send()
                line_arrival(turn, slot).wait_recv()
            else:
                last(slot).wait()


def homeward_kernel(
    bands, src, zeros, dst, mid, plane_send, plane_recv, line_send, line_recv, own_sem, zero_sem
):
    band, field = lax.axis_index("band"), lax.axis_index("field")
    middle = pl.ds(bands // 2 - 1, 2)
    greet(band, field, bands)

    def held(turn, slot, target):
        return src.at[field, slot, target] if turn == 0 else mid.at[turn, slot, target]

    def second_slot(turn, target, act):
        north, south = bands // 4, bands - bands // 4 - 1

        @pl.when(target == north)
        def _():
            act(held(turn, 0, bands - 1))

        @pl.when(target == south)
        def _():
            act(held(turn, 0, 0))

        @pl.when((target > north) & (target < south))
        def _():
            act(held(turn, 1, target))

    def plane(turn, step, slot, source):
        peer = lax.rem(band + step, bands)
        return remote(
            source, dst.at[band, partner(field, turn), slot],
            plane_send.at[turn, step, slot], plane_recv.at[turn, step, slot], (peer, field),
        )

    def arrival(turn, step, slot):
        peer = lax.rem(band + bands - step, bands)
        spot = dst.at[peer, partner(field, turn), slot]
        return remote(
            spot, spot, plane_send.at[turn, step, slot], plane_recv.at[turn, step, slot], (peer, field)
        )

    def own(turn, slot, source):
        return pltpu.make_async_copy(
            source, dst.at[band, partner(field, turn), slot], own_sem.at[turn, slot]
        )

    def blank(peer, z):
        return pltpu.make_async_copy(zeros, dst.at[peer, z, 1], zero_sem.at[peer, z])

    def line(turn, slot):
        goal = partner(field, turn)
        if slot == 0:
            source, target = src.at[goal, 0], mid.at[turn, 0]
        else:
            source, target = src.at[goal, 1, middle], mid.at[turn, 1, middle]
        return remote(
            source, target, line_send.at[turn, slot], line_recv.at[turn, slot], (band, goal)
        )

    def spread(turn):
        @pl.loop(1, bands)
        def _(step):
            peer = lax.rem(band + step, bands)
            plane(turn, step, 0, held(turn, 0, peer)).start()
            second_slot(turn, peer, lambda source: plane(turn, step, 1, source).start())

        own(turn, 0, held(turn, 0, band)).start()
        second_slot(turn, band, lambda source: own(turn, 1, source).start())

    for turn in (2, 1):
        line(turn, 0).start()
        line(turn, 1).start()
    spread(0)

    @pl.when(jnp.logical_not(near_equator(band, bands)))
    def _():
        @pl.loop(0, bands)
        def _(peer):
            for z in range(4):
                blank(peer, z).start()

    for slot in range(2):
        line(2, slot).wait_recv()
        line(3, slot).start()
    spread(2)
    for turn in (1, 3):
        line(turn, 0).wait_recv()
        line(turn, 1).wait_recv()
        spread(turn)

    @pl.when(jnp.logical_not(near_equator(band, bands)))
    def _():
        @pl.loop(0, bands)
        def _(peer):
            for z in range(4):
                blank(peer, z).wait()

    for turn in (0, 2, 1, 3):
        own(turn, 0, held(turn, 0, band)).wait()

        @pl.when(near_equator(band, bands))
        def _():
            own(turn, 1, held(turn, 1, band)).wait()

        @pl.loop(1, bands)
        def _(step):
            peer = lax.rem(band + step, bands)
            plane(turn, step, 0, held(turn, 0, peer)).wait_send()
            arrival(turn, step, 0).wait_recv()
            second_slot(turn, peer, lambda source: plane(turn, step, 1, source).wait_send())

            @pl.when(near_equator(band, bands))
            def _():
                arrival(turn, step, 1).wait_recv()

        if turn:
            line(turn, 0).wait_send()
            line(turn, 1).wait_send()


def staged_scratch(bands, piece):
    return [
        pltpu.VMEM((4, 2, bands) + piece, jnp.bfloat16),
        pltpu.SemaphoreType.DMA((4, bands, 2)),
        pltpu.SemaphoreType.DMA((4, bands, 2)),
        pltpu.SemaphoreType.DMA((4, 2)),
        pltpu.SemaphoreType.DMA((4, 2)),
        pltpu.SemaphoreType.DMA((4, 2)),
    ]


def outward(data):
    bands, fields, _, count, width = data.shape
    return pl.pallas_call(
        functools.partial(outward_kernel, bands),
        out_shape=jax.ShapeDtypeStruct((fields, 2, bands, count, width), data.dtype),
        in_specs=[pl.BlockSpec(memory_space=pl.ANY)],
        out_specs=pl.BlockSpec(memory_space=pl.ANY),
        scratch_shapes=staged_scratch(bands, (count, width)) + [pltpu.SemaphoreType.DMA((2,))],
        compiler_params=pltpu.CompilerParams(
            collective_id=0, has_side_effects=True, vmem_limit_bytes=12 * 1024 * 1024
        ),
    )(data)


def homeward(data):
    fields, _, bands, count, width = data.shape
    return pl.pallas_call(
        functools.partial(homeward_kernel, bands),
        out_shape=jax.ShapeDtypeStruct((bands, fields, 2, count, width), data.dtype),
        in_specs=[pl.BlockSpec(memory_space=pl.ANY)] * 2,
        out_specs=pl.BlockSpec(memory_space=pl.ANY),
        scratch_shapes=staged_scratch(bands, (count, width)) + [pltpu.SemaphoreType.DMA((bands, 4))],
        compiler_params=pltpu.CompilerParams(
            collective_id=1, has_side_effects=True, vmem_limit_bytes=12 * 1024 * 1024
        ),
    )(data, jnp.zeros((count, width), data.dtype))


def compact_table(waves, first_wave, table, spare, shared):
    rows, half = table.shape
    boundary = waves - first_wave
    row_ids = lax.broadcasted_iota(jnp.int32, (rows, half), 0)
    lanes = lax.broadcasted_iota(jnp.int32, (rows, half), 1)
    held = row_ids < boundary
    degree = jnp.where(held, row_ids, row_ids - boundary)
    even = degree % 2 == 0
    up = lax.broadcasted_iota(jnp.int32, (half, half), 0)
    across = lax.broadcasted_iota(jnp.int32, (half, half), 1)
    turn = (up + across == half - 1).astype(jnp.float32).astype(jnp.bfloat16)
    origin = jnp.where(across < half // 2, across + half // 2, half + half // 2 - 1 - across)
    halved = (up == origin).astype(jnp.float32).astype(jnp.bfloat16)
    northern = table.astype(jnp.float32)
    zero = jnp.zeros((), jnp.float32)
    second = jnp.where(held, zero, northern)
    reach = 2 * half // 16 + waves // half * lanes
    mates = (lanes < half // 4) & (first_wave >= reach)
    mirror = (up + across == half - half // 4 - 1).astype(jnp.float32).astype(jnp.bfloat16)
    second_rows = second.astype(jnp.bfloat16)
    mirrored = jnp.dot(second_rows, mirror, preferred_element_type=jnp.float32)
    moved = (lanes == spare) & (first_wave >= waves // 2 - 8)
    main = jnp.where(moved, second[:, shared : shared + 1], jnp.where(held, northern, zero))
    main = jnp.where(mates, mirrored, main)
    southern = jnp.dot(main.astype(jnp.bfloat16), turn, preferred_element_type=jnp.float32)
    main = jnp.where(mates & jnp.logical_not(even), -main, main).astype(jnp.bfloat16)
    from_pole = half - 1 - lanes
    mates = (from_pole < half // 4) & (first_wave >= 2 * half // 16 + waves // half * from_pole)
    southern = jnp.where(even | mates, southern, -southern)
    extra = jnp.dot(second_rows, halved, preferred_element_type=jnp.float32)
    extra = jnp.where(even | (lanes < half // 2), extra, -extra)
    return jnp.concatenate([main, southern.astype(jnp.bfloat16), extra.astype(jnp.bfloat16)], axis=1)


def packed_kernel(waves, lats, spare, shared, first, x_ref, table_ref, mix_ref, out_ref, held_ref):
    k = pl.program_id(0)
    fields, _, bands, count, width = x_ref.shape
    tiles = width // 128
    group = 128 // lats
    rows = fields * tiles
    low, high = bands // 4, bands - bands // 4
    spans = [(0, 0, bands, 0), (1, low + 1, high - 1, bands + 1)]

    @pl.when(k == 0)
    def _():
        held_ref[bands] = jnp.zeros(held_ref.shape[1:], jnp.float32)
        held_ref[bands + high - low - 1] = jnp.zeros(held_ref.shape[1:], jnp.float32)
        for slot, begin, end, base in spans:

            @pl.loop(begin, end)
            def _(band):
                for field in range(fields):
                    for tile in range(tiles):
                        at = (field * tiles + tile) * count
                        held_ref[base - begin + band, at : at + count, :] = x_ref[
                            field, slot, band, :, tile * 128 : (tile + 1) * 128
                        ].astype(jnp.float32)

    place = pl.ds(k, rows, stride=count)
    slabs = bands + high - low
    gathered = [[] for _ in range(group)]
    for start in range(0, slabs, group):
        parts = [held_ref[start + i, place, :] for i in range(group)]
        for j, part in enumerate(swap_groups(parts, lats)):
            gathered[j].append(part)
    values = jnp.concatenate([jnp.concatenate(g, axis=1) for g in gathered], axis=0).astype(jnp.bfloat16)
    full = compact_table(waves, first[k], table_ref[0], spare, shared)
    result = there_and_back(values, full, mix_ref[...])
    for start in range(0, slabs, group):
        at = start * lats
        parts = [result[j * rows : (j + 1) * rows, at : at + 128] for j in range(group)]
        for i, part in enumerate(swap_groups(parts, lats)):
            held_ref[start + i, place, :] = part

    @pl.when(k == pl.num_programs(0) - 1)
    def _():
        for slot, begin, end, base in spans:

            @pl.loop(begin, end)
            def _(band):
                for field in range(fields):
                    for tile in range(tiles):
                        at = (field * tiles + tile) * count
                        out_ref[field, slot, band, :, tile * 128 : (tile + 1) * 128] = held_ref[
                            base - begin + band, at : at + count, :
                        ].astype(jnp.bfloat16)


def packed_transform(arrived, legendre, mixing, pair_first, waves, lats, spare, shared):
    fields, _, bands, count, width = arrived.shape
    pairs, rows, half = legendre.shape
    columns = mixing.shape[0]
    flops = 2 * pairs * columns * rows * (3 * bands * lats + columns)
    whole = pl.BlockSpec(arrived.shape, lambda k, first: (0, 0, 0, 0, 0))
    slabs = bands + bands - 2 * (bands // 4)
    return pl.pallas_call(
        functools.partial(packed_kernel, waves, lats, spare, shared),
        grid_spec=pltpu.PrefetchScalarGridSpec(
            num_scalar_prefetch=1,
            grid=(pairs,),
            in_specs=[
                whole,
                pl.BlockSpec((1, rows, half), lambda k, first: (k, 0, 0)),
                pl.BlockSpec((columns, columns), lambda k, first: (0, 0)),
            ],
            out_specs=whole,
            scratch_shapes=[pltpu.VMEM((slabs, fields * width // 128 * count, 128), jnp.float32)],
        ),
        out_shape=jax.ShapeDtypeStruct(arrived.shape, jnp.bfloat16),
        compiler_params=pltpu.CompilerParams(vmem_limit_bytes=52 * 1024 * 1024),
        cost_estimate=pl.CostEstimate(
            flops=flops, bytes_accessed=4 * arrived.size + 2 * legendre.size, transcendentals=0
        ),
    )(pair_first, arrived, legendre, mixing)


def mixing_by_rows(vertical, fields, group):
    levels = vertical.shape[1]
    per_field = 2 * levels // fields
    tiles = 2 * per_field // group
    j, z, t = np.meshgrid(np.arange(group), np.arange(fields), np.arange(tiles), indexing="ij")
    column = (t * group + j).reshape(-1)
    part = column // per_field
    level = z.reshape(-1) * per_field + column % per_field
    rows = level.size
    choose = np.zeros((2, rows, levels), np.float32)
    choose[level // levels, np.arange(rows), level % levels] = 1
    choose = jnp.asarray(choose, jnp.bfloat16)
    left = jnp.einsum("qra,qab->rqb", choose, vertical, preferred_element_type=jnp.float32)
    both = jnp.einsum(
        "rqb,qsb->rs", left.astype(jnp.bfloat16), choose, preferred_element_type=jnp.float32
    )
    return jnp.where(jnp.asarray(part[:, None] == part[None, :]), both, 0.0).astype(jnp.bfloat16)


def mixing_matrix(vertical, fields):
    levels = vertical.shape[1]
    total = 2 * levels
    blocks = jnp.zeros((2, levels, 2, levels), vertical.dtype)
    blocks = blocks.at[0, :, 0, :].set(vertical[0]).at[1, :, 1, :].set(vertical[1])
    block = blocks.reshape(fields, total // fields, fields, total // fields)
    parts = jnp.eye(2, dtype=vertical.dtype)
    return jnp.einsum("zfyg,cd->zcfydg", block, parts).reshape(2 * total, 2 * total)


def spread_waves(choose, masked):
    levels, lats, _, waves = masked.shape
    flat = masked.transpose(2, 0, 1, 3).reshape(2 * levels * lats, waves)
    return lax.dot_general(
        choose, flat, (((1,), (1,)), ((), ())), preferred_element_type=jnp.float32
    ).astype(jnp.bfloat16)


def gather_waves(home, choose, shape):
    levels, lats, _, waves = shape
    restored = lax.dot_general(
        home, choose, (((0,), (0,)), ((), ())), preferred_element_type=jnp.float32
    ).astype(jnp.bfloat16)
    return restored.reshape(2, levels, lats, waves).transpose(1, 2, 0, 3)


def per_device(fourier, row_length, wave_order, legendre, vertical):
    levels, lats, _, waves = fourier.shape
    bands, fields = lax.axis_size("band"), lax.axis_size("field")
    band = lax.axis_index("band")
    total = bands * fields
    pairs, _, half = legendre.shape
    wave_ids = lax.iota(jnp.int32, waves)
    wave_count = jnp.minimum(waves, row_length // 2)
    in_range = (wave_ids[None, :] < wave_count[:, None])[None, :, None, :]
    nothing = jnp.zeros((), jnp.bfloat16)
    masked = jnp.where(in_range, fourier, nothing)
    start_pair = (band * fields + lax.axis_index("field")) * pairs
    pair_first = lax.dynamic_slice_in_dim(wave_order, start_pair, pairs)
    width = 2 * levels * lats

    if (bands, fields, lats, half, waves, pairs, levels) == (8, 4, 32, 128, 1024, 16, 36):
        spare, shared, edge = half // 4, half // 2 - 1, waves // 2
        turned = band >= bands // 2
        in_band = (band == 1) | (band == bands - 2)
        spare_lat = jnp.where(turned, lats - 1, 0)
        shared_lat = jnp.where(turned, 0, lats - 1)
        lat_ids = lax.iota(jnp.int32, lats)[None, :, None, None]
        wave_at = wave_ids[None, None, None, :]
        to_spare = in_band & (lat_ids == spare_lat) & (wave_at >= edge - 8) & (wave_at < edge)
        to_shared = in_band & (lat_ids == shared_lat) & (wave_at >= edge) & (wave_at < edge + 8)
        row = lax.dynamic_slice_in_dim(fourier, shared_lat, 1, axis=1)[..., edge : edge + 8]
        count = lax.dynamic_slice_in_dim(wave_count, shared_lat, 1, axis=0)
        row = jnp.where(wave_ids[edge : edge + 8] < count[0], row, nothing)
        pad = ((0, 0), (0, 0), (0, 0), (edge - 8, waves - edge))
        masked = jnp.where(to_spare, jnp.pad(jnp.flip(row, 3), pad), masked)

        by_holder = wave_order.reshape(total, pairs)
        ordering = jnp.concatenate([by_holder, waves - 1 - by_holder], axis=1).reshape(waves)
        choose = (ordering[:, None] == wave_ids[None, :]).astype(jnp.bfloat16)
        outgoing = spread_waves(choose, masked).reshape(bands, fields, 2, pairs, width)
        mixing = mixing_by_rows(vertical, fields, 128 // lats)
        back = packed_transform(
            outward(outgoing), legendre, mixing, pair_first, waves, lats, spare, shared
        )
        restored = gather_waves(homeward(back).reshape(waves, width), choose, fourier.shape)
        row = lax.dynamic_slice_in_dim(restored, spare_lat, 1, axis=1)[..., edge - 8 : edge]
        pad = ((0, 0), (0, 0), (0, 0), (edge, waves - edge - 8))
        restored = jnp.where(to_shared, jnp.pad(jnp.flip(row, 3), pad), restored)
        return jnp.where(in_range, restored, nothing)

    ordering = jnp.stack([wave_order, waves - 1 - wave_order], axis=1).reshape(waves)
    choose = (ordering[:, None] == wave_ids[None, :]).astype(jnp.bfloat16)
    outgoing = spread_waves(choose, masked)
    arrived = exchange(outgoing.reshape(total, 2 * pairs, width), bands, fields, 2)
    values = arrived.reshape(bands, fields, pairs, 2, 2 * levels, lats).transpose(2, 1, 4, 3, 0, 5)
    values = values.reshape(pairs, fields * 2 * levels, 2 * bands * lats)
    grid_part = transform(values, legendre, mixing_matrix(vertical, fields), pair_first, waves)
    back = grid_part.reshape(pairs, fields, 2 * levels, 2, bands, lats).transpose(4, 1, 0, 3, 2, 5)
    home = exchange(back.reshape(total, 2 * pairs, width), bands, fields, 3)
    return jnp.where(in_range, gather_waves(home.reshape(waves, width), choose, fourier.shape), nothing)


def solution(mesh):
    placed = (P("field", "band", None, None), P("band"), P(), P(("band", "field"), None, None), P())
    return jax.shard_map(
        per_device,
        mesh=mesh,
        in_specs=placed,
        out_specs=P("field", "band", None, None),
        check_vma=False,
    )
```

```python
import functools

import jax
import jax.numpy as jnp
import numpy as np
from jax import lax
from jax.experimental import pallas as pl
from jax.experimental.pallas import tpu as pltpu
from jax.sharding import PartitionSpec as P

MESH = pl.DeviceIdType.MESH


def exchange_kernel(bands, fields, src, dst, send_sem, recv_sem, own_sem):
    total = bands * fields
    band, field = lax.axis_index("band"), lax.axis_index("field")
    me = band * fields + field

    def other(step):
        peer = lax.rem(me + step, total)
        return peer, (peer // fields, lax.rem(peer, fields))

    barrier = pltpu.get_barrier_semaphore()

    @pl.loop(1, total)
    def _(step):
        _, where = other(step)
        pl.semaphore_signal(barrier, inc=1, device_id=where, device_id_type=MESH)

    own = pltpu.make_async_copy(src.at[me], dst.at[me], own_sem)
    own.start()
    pl.semaphore_wait(barrier, total - 1)

    def copy(step):
        peer, where = other(step)
        return pltpu.make_async_remote_copy(
            src_ref=src.at[peer],
            dst_ref=dst.at[me],
            send_sem=send_sem.at[step],
            recv_sem=recv_sem.at[step],
            device_id=where,
            device_id_type=MESH,
        )

    @pl.loop(1, total)
    def _(step):
        copy(step).start()

    @pl.loop(1, total)
    def _(step):
        copy(step).wait_send()
        peer = lax.rem(me + total - step, total)
        pltpu.make_async_remote_copy(
            src_ref=src.at[peer],
            dst_ref=dst.at[peer],
            send_sem=send_sem.at[step],
            recv_sem=recv_sem.at[step],
            device_id=(peer // fields, lax.rem(peer, fields)),
            device_id_type=MESH,
        ).wait_recv()

    own.wait()


def exchange(data, bands, fields, ident):
    total = bands * fields
    return pl.pallas_call(
        functools.partial(exchange_kernel, bands, fields),
        out_shape=jax.ShapeDtypeStruct(data.shape, data.dtype),
        in_specs=[pl.BlockSpec(memory_space=pl.ANY)],
        out_specs=pl.BlockSpec(memory_space=pl.ANY),
        scratch_shapes=[
            pltpu.SemaphoreType.DMA((total,)),
            pltpu.SemaphoreType.DMA((total,)),
            pltpu.SemaphoreType.DMA,
        ],
        compiler_params=pltpu.CompilerParams(collective_id=ident, has_side_effects=True),
    )(data)


def pair_kernel(waves, first, x_ref, table_ref, mix_ref, out_ref):
    full = masked_table(waves, first[pl.program_id(0)], table_ref[0])
    out_ref[0] = there_and_back(x_ref[0], full, mix_ref[...]).astype(jnp.bfloat16)


def transform(values, legendre, mixing, pair_first, waves):
    pairs, columns, span = values.shape
    rows, half = legendre.shape[1:]
    flops = 2 * pairs * columns * rows * (2 * span + columns)
    return pl.pallas_call(
        functools.partial(pair_kernel, waves),
        grid_spec=pltpu.PrefetchScalarGridSpec(
            num_scalar_prefetch=1,
            grid=(pairs,),
            in_specs=[
                pl.BlockSpec((1, columns, span), lambda k, first: (k, 0, 0)),
                pl.BlockSpec((1, rows, half), lambda k, first: (k, 0, 0)),
                pl.BlockSpec((columns, columns), lambda k, first: (0, 0)),
            ],
            out_specs=pl.BlockSpec((1, columns, span), lambda k, first: (k, 0, 0)),
        ),
        out_shape=jax.ShapeDtypeStruct(values.shape, jnp.bfloat16),
        compiler_params=pltpu.CompilerParams(vmem_limit_bytes=48 * 1024 * 1024),
        cost_estimate=pl.CostEstimate(
            flops=flops, bytes_accessed=4 * values.size + 2 * legendre.size, transcendentals=0
        ),
    )(pair_first, values, legendre, mixing)


def swap_groups(parts, lats):
    lane_group = lax.broadcasted_iota(jnp.int32, parts[0].shape, 1) // lats
    swapped = []
    for j in range(len(parts)):
        merged = None
        for i, part in enumerate(parts):
            shift = ((i - j) * lats) % 128
            turned = pltpu.roll(part, shift, 1) if shift else part
            merged = turned if merged is None else jnp.where(lane_group == i, turned, merged)
        swapped.append(merged)
    return swapped


def masked_table(waves, first_wave, table):
    rows, half = table.shape
    boundary = waves - first_wave
    up = lax.broadcasted_iota(jnp.int32, (half, half), 0)
    across = lax.broadcasted_iota(jnp.int32, (half, half), 1)
    turn = (up + across == half - 1).astype(jnp.float32).astype(jnp.bfloat16)
    southern = jnp.dot(table, turn, preferred_element_type=jnp.float32)
    northern = table.astype(jnp.float32)
    row_ids = lax.broadcasted_iota(jnp.int32, (rows, half), 0)
    held = row_ids < boundary
    degree = jnp.where(held, row_ids, row_ids - boundary)
    southern = jnp.where(degree % 2 == 0, southern, -southern)
    zero = jnp.zeros((), jnp.float32)
    return jnp.concatenate(
        [
            jnp.where(held, northern, zero).astype(jnp.bfloat16),
            jnp.where(held, southern, zero).astype(jnp.bfloat16),
            jnp.where(held, zero, northern).astype(jnp.bfloat16),
            jnp.where(held, zero, southern).astype(jnp.bfloat16),
        ],
        axis=1,
    )


def there_and_back(values, full, mixing):
    spectral = lax.dot_general(
        values, full, (((1,), (1,)), ((), ())), preferred_element_type=jnp.float32
    ).astype(jnp.bfloat16)
    updated = jnp.dot(mixing, spectral, preferred_element_type=jnp.float32).astype(jnp.bfloat16)
    return jnp.dot(updated, full, preferred_element_type=jnp.float32)


ROUNDS = (2, 3, 1, 0)


def partner(field, turn):
    if turn == 0:
        return field
    if turn == 2:
        return lax.rem(field + 2, 4)
    return 3 - field if turn == 3 else field + 1 - 2 * lax.rem(field, 2)


def near_equator(band, bands):
    return (band >= bands // 4) & (band < bands - bands // 4)


def greet(band, field, bands):
    barrier = pltpu.get_barrier_semaphore()

    @pl.loop(1, bands)
    def _(step):
        where = (lax.rem(band + step, bands), field)
        pl.semaphore_signal(barrier, inc=1, device_id=where, device_id_type=MESH)

    for turn in (1, 2, 3):
        where = (band, partner(field, turn))
        pl.semaphore_signal(barrier, inc=1, device_id=where, device_id_type=MESH)
    pl.semaphore_wait(barrier, bands - 1 + 3)


def remote(src, dst, send, recv, where):
    return pltpu.make_async_remote_copy(
        src_ref=src, dst_ref=dst, send_sem=send, recv_sem=recv, device_id=where, device_id_type=MESH
    )


def outward_kernel(bands, src, dst, mid, plane_send, plane_recv, line_send, line_recv, own_sem, last_sem):
    band, field = lax.axis_index("band"), lax.axis_index("field")
    middle = pl.ds(bands // 2 - 1, 2)
    greet(band, field, bands)

    def plane(turn, step, slot):
        peer = lax.rem(band + step, bands)
        return remote(
            src.at[peer, partner(field, turn), slot], mid.at[turn, slot, band],
            plane_send.at[turn, step, slot], plane_recv.at[turn, step, slot], (peer, field),
        )

    def arrival(turn, step, slot):
        peer = lax.rem(band + bands - step, bands)
        spot = mid.at[turn, slot, peer]
        return remote(
            spot, spot, plane_send.at[turn, step, slot], plane_recv.at[turn, step, slot], (peer, field)
        )

    def own(turn, slot):
        return pltpu.make_async_copy(
            src.at[band, partner(field, turn), slot], mid.at[turn, slot, band], own_sem.at[turn, slot]
        )

    def ends(turn, slot, origin):
        if slot == 0:
            return mid.at[turn, 0], dst.at[origin, 0]
        return mid.at[turn, 1, middle], dst.at[origin, 1, middle]

    def line(turn, slot):
        source, target = ends(turn, slot, field)
        where = (band, partner(field, turn))
        return remote(source, target, line_send.at[turn, slot], line_recv.at[turn, slot], where)

    def line_arrival(turn, slot):
        origin = partner(field, turn)
        spot = ends(turn, slot, origin)[1]
        return remote(
            spot, spot, line_send.at[turn, slot], line_recv.at[turn, slot], (band, origin)
        )

    def last(slot):
        source, target = ends(0, slot, field)
        return pltpu.make_async_copy(source, target, last_sem.at[slot])

    def begin(turn):
        own(turn, 0).start()
        own(turn, 1).start()

        @pl.loop(1, bands)
        def _(step):
            plane(turn, step, 0).start()

            @pl.when(near_equator(band, bands))
            def _():
                plane(turn, step, 1).start()

    begin(ROUNDS[0])
    for at, turn in enumerate(ROUNDS):
        own(turn, 0).wait()
        own(turn, 1).wait()

        @pl.loop(1, bands)
        def _(step):
            arrival(turn, step, 0).wait_recv()

            @pl.when(near_equator(lax.rem(band + bands - step, bands), bands))
            def _():
                arrival(turn, step, 1).wait_recv()

        if at + 1 < len(ROUNDS):
            begin(ROUNDS[at + 1])
        for pole, mate in ((0, bands - bands // 4 - 1), (bands - 1, bands // 4)):
            mid[turn, 0, pole] = mid[turn, 0, pole] + mid[turn, 1, mate]
        for slot in range(2):
            if turn:
                line(turn, slot).start()
            else:
                last(slot).start()

    for turn in ROUNDS:

        @pl.loop(1, bands)
        def _(step):
            plane(turn, step, 0).wait_send()

            @pl.when(near_equator(band, bands))
            def _():
                plane(turn, step, 1).wait_send()

        for slot in range(2):
            if turn:
                line(turn, slot).wait_send()
                line_arrival(turn, slot).wait_recv()
            else:
                last(slot).wait()


def homeward_kernel(
    bands, src, zeros, dst, mid, plane_send, plane_recv, line_send, line_recv, own_sem, zero_sem
):
    band, field = lax.axis_index("band"), lax.axis_index("field")
    middle = pl.ds(bands // 2 - 1, 2)
    greet(band, field, bands)

    def held(turn, slot, target):
        return src.at[field, slot, target] if turn == 0 else mid.at[turn, slot, target]

    def second_slot(turn, target, act):
        north, south = bands // 4, bands - bands // 4 - 1

        @pl.when(target == north)
        def _():
            act(held(turn, 0, bands - 1))

        @pl.when(target == south)
        def _():
            act(held(turn, 0, 0))

        @pl.when((target > north) & (target < south))
        def _():
            act(held(turn, 1, target))

    def plane(turn, step, slot, source):
        peer = lax.rem(band + step, bands)
        return remote(
            source, dst.at[band, partner(field, turn), slot],
            plane_send.at[turn, step, slot], plane_recv.at[turn, step, slot], (peer, field),
        )

    def arrival(turn, step, slot):
        peer = lax.rem(band + bands - step, bands)
        spot = dst.at[peer, partner(field, turn), slot]
        return remote(
            spot, spot, plane_send.at[turn, step, slot], plane_recv.at[turn, step, slot], (peer, field)
        )

    def own(turn, slot, source):
        return pltpu.make_async_copy(
            source, dst.at[band, partner(field, turn), slot], own_sem.at[turn, slot]
        )

    def blank(peer, z):
        return pltpu.make_async_copy(zeros, dst.at[peer, z, 1], zero_sem.at[peer, z])

    def line(turn, slot):
        goal = partner(field, turn)
        if slot == 0:
            source, target = src.at[goal, 0], mid.at[turn, 0]
        else:
            source, target = src.at[goal, 1, middle], mid.at[turn, 1, middle]
        return remote(
            source, target, line_send.at[turn, slot], line_recv.at[turn, slot], (band, goal)
        )

    def spread(turn):
        @pl.loop(1, bands)
        def _(step):
            peer = lax.rem(band + step, bands)
            plane(turn, step, 0, held(turn, 0, peer)).start()
            second_slot(turn, peer, lambda source: plane(turn, step, 1, source).start())

        own(turn, 0, held(turn, 0, band)).start()
        second_slot(turn, band, lambda source: own(turn, 1, source).start())

    for turn in (2, 1):
        line(turn, 0).start()
        line(turn, 1).start()
    spread(0)

    @pl.when(jnp.logical_not(near_equator(band, bands)))
    def _():
        @pl.loop(0, bands)
        def _(peer):
            for z in range(4):
                blank(peer, z).start()

    for slot in range(2):
        line(2, slot).wait_recv()
        line(3, slot).start()
    spread(2)
    for turn in (1, 3):
        line(turn, 0).wait_recv()
        line(turn, 1).wait_recv()
        spread(turn)

    @pl.when(jnp.logical_not(near_equator(band, bands)))
    def _():
        @pl.loop(0, bands)
        def _(peer):
            for z in range(4):
                blank(peer, z).wait()

    for turn in (0, 2, 1, 3):
        own(turn, 0, held(turn, 0, band)).wait()

        @pl.when(near_equator(band, bands))
        def _():
            own(turn, 1, held(turn, 1, band)).wait()

        @pl.loop(1, bands)
        def _(step):
            peer = lax.rem(band + step, bands)
            plane(turn, step, 0, held(turn, 0, peer)).wait_send()
            arrival(turn, step, 0).wait_recv()
            second_slot(turn, peer, lambda source: plane(turn, step, 1, source).wait_send())

            @pl.when(near_equator(band, bands))
            def _():
                arrival(turn, step, 1).wait_recv()

        if turn:
            line(turn, 0).wait_send()
            line(turn, 1).wait_send()


def staged_scratch(bands, piece):
    return [
        pltpu.VMEM((4, 2, bands) + piece, jnp.bfloat16),
        pltpu.SemaphoreType.DMA((4, bands, 2)),
        pltpu.SemaphoreType.DMA((4, bands, 2)),
        pltpu.SemaphoreType.DMA((4, 2)),
        pltpu.SemaphoreType.DMA((4, 2)),
        pltpu.SemaphoreType.DMA((4, 2)),
    ]


def outward(data):
    bands, fields, _, count, width = data.shape
    return pl.pallas_call(
        functools.partial(outward_kernel, bands),
        out_shape=jax.ShapeDtypeStruct((fields, 2, bands, count, width), data.dtype),
        in_specs=[pl.BlockSpec(memory_space=pl.ANY)],
        out_specs=pl.BlockSpec(memory_space=pl.ANY),
        scratch_shapes=staged_scratch(bands, (count, width)) + [pltpu.SemaphoreType.DMA((2,))],
        compiler_params=pltpu.CompilerParams(
            collective_id=0, has_side_effects=True, vmem_limit_bytes=12 * 1024 * 1024
        ),
    )(data)


def homeward(data):
    fields, _, bands, count, width = data.shape
    return pl.pallas_call(
        functools.partial(homeward_kernel, bands),
        out_shape=jax.ShapeDtypeStruct((bands, fields, 2, count, width), data.dtype),
        in_specs=[pl.BlockSpec(memory_space=pl.ANY)] * 2,
        out_specs=pl.BlockSpec(memory_space=pl.ANY),
        scratch_shapes=staged_scratch(bands, (count, width)) + [pltpu.SemaphoreType.DMA((bands, 4))],
        compiler_params=pltpu.CompilerParams(
            collective_id=1, has_side_effects=True, vmem_limit_bytes=12 * 1024 * 1024
        ),
    )(data, jnp.zeros((count, width), data.dtype))


def lane_origins(half):
    lane = np.arange(half)
    columns = [
        half - 1 - lane,
        np.where(lane < half // 2, lane + half // 2, half + half // 2 - 1 - lane),
        half - half // 4 - 1 - lane,
        lane - half // 4,
    ]
    return (np.arange(half)[:, None] == np.concatenate(columns)[None, :]).astype(np.float32)


def compact_table(waves, first_wave, table, select, spare):
    rows, half = table.shape
    boundary = waves - first_wave
    row_ids = lax.broadcasted_iota(jnp.int32, (rows, half), 0)
    lanes = lax.broadcasted_iota(jnp.int32, (1, half), 1)
    held = row_ids < boundary
    degree = jnp.where(held, row_ids, row_ids - boundary)
    sign = (1 - 2 * (degree % 2)).astype(jnp.float32)
    variants = jnp.dot(table.astype(jnp.bfloat16), select, preferred_element_type=jnp.float32)
    turned, extra, mirrored, mirrored_south = [
        variants[:, i * half : (i + 1) * half] for i in range(4)
    ]

    def shares(from_pole):
        mates = (from_pole < half // 4) & (first_wave >= half // 8 + waves // half * from_pole)
        moved = (from_pole == spare) & (first_wave >= waves // 2 - 8)
        mates, moved = mates.astype(jnp.float32), moved.astype(jnp.float32)
        return mates, moved, 1.0 - mates - moved

    mates, moved, kept = shares(lanes)
    main = jnp.where(held, table * kept, mirrored * (sign * mates + moved))
    mates, moved, kept = shares(half - 1 - lanes)
    southern = jnp.where(held, turned * (sign * kept), mirrored_south * (mates + sign * moved))
    upper = (lanes < half // 2).astype(jnp.float32)
    extra = jnp.where(held, 0.0, extra * (upper + sign * (1.0 - upper)))
    return jnp.concatenate([main, southern, extra], axis=1).astype(jnp.bfloat16)


def packed_kernel(
    waves, lats, spare, first, x_ref, table_ref, mix_ref, select_ref, out_ref, held_ref, wide_ref
):
    k = pl.program_id(0)
    fields, _, bands, count, width = x_ref.shape
    tiles = width // 128
    group = 128 // lats
    rows = fields * tiles
    low, high = bands // 4, bands - bands // 4
    spans = [(0, 0, bands, 0), (1, low + 1, high - 1, bands + 1)]

    @pl.when(k == 0)
    def _():
        row_total, pairs, half = table_ref.shape
        step = next(n for n in range(32, 0, -1) if row_total % n == 0)

        @pl.loop(0, row_total // step)
        def _(i):
            block = table_ref[pl.ds(i * step, step)].astype(jnp.float32)
            at = pl.multiple_of(i * (step * pairs), step * pairs)
            wide_ref[pl.ds(at, step * pairs), :] = block.reshape(step * pairs, half)

        held_ref[bands] = jnp.zeros(held_ref.shape[1:], jnp.float32)
        held_ref[bands + high - low - 1] = jnp.zeros(held_ref.shape[1:], jnp.float32)
        for slot, begin, end, base in spans:

            @pl.loop(begin, end)
            def _(band):
                for field in range(fields):
                    for tile in range(tiles):
                        at = (field * tiles + tile) * count
                        held_ref[base - begin + band, at : at + count, :] = x_ref[
                            field, slot, band, :, tile * 128 : (tile + 1) * 128
                        ].astype(jnp.float32)

    place = pl.ds(k, rows, stride=count)
    slabs = bands + high - low
    gathered = [[] for _ in range(group)]
    for start in range(0, slabs, group):
        parts = [held_ref[start + i, place, :] for i in range(group)]
        for j, part in enumerate(swap_groups(parts, lats)):
            gathered[j].append(part)
    values = jnp.concatenate([jnp.concatenate(g, axis=1) for g in gathered], axis=0).astype(jnp.bfloat16)
    table = wide_ref[pl.ds(k, table_ref.shape[0], stride=table_ref.shape[1]), :]
    full = compact_table(waves, first[k], table, select_ref[...], spare)
    mixed = jnp.dot(mix_ref[...], values, preferred_element_type=jnp.float32).astype(jnp.bfloat16)
    updated = lax.dot_general(
        mixed, full, (((1,), (1,)), ((), ())), preferred_element_type=jnp.float32
    ).astype(jnp.bfloat16)
    result = jnp.dot(updated, full, preferred_element_type=jnp.float32)
    for start in range(0, slabs, group):
        at = start * lats
        parts = [result[j * rows : (j + 1) * rows, at : at + 128] for j in range(group)]
        for i, part in enumerate(swap_groups(parts, lats)):
            held_ref[start + i, place, :] = part

    @pl.when(k == pl.num_programs(0) - 1)
    def _():
        for slot, begin, end, base in spans:

            @pl.loop(begin, end)
            def _(band):
                for field in range(fields):
                    for tile in range(tiles):
                        at = (field * tiles + tile) * count
                        out_ref[field, slot, band, :, tile * 128 : (tile + 1) * 128] = held_ref[
                            base - begin + band, at : at + count, :
                        ].astype(jnp.bfloat16)


def packed_transform(arrived, legendre, mixing, pair_first, waves, lats, spare):
    fields, _, bands, count, width = arrived.shape
    pairs, rows, half = legendre.shape
    columns = mixing.shape[0]
    flops = 2 * pairs * columns * rows * (3 * bands * lats + columns)
    whole = pl.BlockSpec(arrived.shape, lambda k, first: (0, 0, 0, 0, 0))
    slabs = bands + bands - 2 * (bands // 4)
    select = jnp.asarray(lane_origins(half), jnp.bfloat16)
    return pl.pallas_call(
        functools.partial(packed_kernel, waves, lats, spare),
        grid_spec=pltpu.PrefetchScalarGridSpec(
            num_scalar_prefetch=1,
            grid=(pairs,),
            in_specs=[
                whole,
                pl.BlockSpec((rows, pairs, half), lambda k, first: (0, 0, 0)),
                pl.BlockSpec((columns, columns), lambda k, first: (0, 0)),
                pl.BlockSpec(select.shape, lambda k, first: (0, 0)),
            ],
            out_specs=whole,
            scratch_shapes=[
                pltpu.VMEM((slabs, fields * width // 128 * count, 128), jnp.float32),
                pltpu.VMEM((rows * pairs, half), jnp.float32),
            ],
        ),
        out_shape=jax.ShapeDtypeStruct(arrived.shape, jnp.bfloat16),
        compiler_params=pltpu.CompilerParams(vmem_limit_bytes=56 * 1024 * 1024),
        cost_estimate=pl.CostEstimate(
            flops=flops, bytes_accessed=4 * arrived.size + 2 * legendre.size, transcendentals=0
        ),
    )(pair_first, arrived, legendre.transpose(1, 0, 2), mixing, select)


def mixing_by_rows(vertical, fields, group):
    levels = vertical.shape[1]
    per_field = 2 * levels // fields
    tiles = 2 * per_field // group
    j, z, t = np.meshgrid(np.arange(group), np.arange(fields), np.arange(tiles), indexing="ij")
    column = (t * group + j).reshape(-1)
    part = column // per_field
    level = z.reshape(-1) * per_field + column % per_field
    rows = level.size
    choose = np.zeros((2, rows, levels), np.float32)
    choose[level // levels, np.arange(rows), level % levels] = 1
    choose = jnp.asarray(choose, jnp.bfloat16)
    left = jnp.einsum("qra,qab->rqb", choose, vertical, preferred_element_type=jnp.float32)
    both = jnp.einsum(
        "rqb,qsb->rs", left.astype(jnp.bfloat16), choose, preferred_element_type=jnp.float32
    )
    return jnp.where(jnp.asarray(part[:, None] == part[None, :]), both, 0.0).astype(jnp.bfloat16)


def mixing_matrix(vertical, fields):
    levels = vertical.shape[1]
    total = 2 * levels
    blocks = jnp.zeros((2, levels, 2, levels), vertical.dtype)
    blocks = blocks.at[0, :, 0, :].set(vertical[0]).at[1, :, 1, :].set(vertical[1])
    block = blocks.reshape(fields, total // fields, fields, total // fields)
    parts = jnp.eye(2, dtype=vertical.dtype)
    return jnp.einsum("zfyg,cd->zcfydg", block, parts).reshape(2 * total, 2 * total)


def spread_waves(choose, masked):
    levels, lats, _, waves = masked.shape
    flat = masked.transpose(2, 0, 1, 3).reshape(2 * levels * lats, waves)
    return lax.dot_general(
        choose, flat, (((1,), (1,)), ((), ())), preferred_element_type=jnp.float32
    ).astype(jnp.bfloat16)


def gather_waves(home, choose, shape):
    levels, lats, _, waves = shape
    restored = lax.dot_general(
        home, choose, (((0,), (0,)), ((), ())), preferred_element_type=jnp.float32
    ).astype(jnp.bfloat16)
    return restored.reshape(2, levels, lats, waves).transpose(1, 2, 0, 3)


def per_device(fourier, row_length, wave_order, legendre, vertical):
    levels, lats, _, waves = fourier.shape
    bands, fields = lax.axis_size("band"), lax.axis_size("field")
    band = lax.axis_index("band")
    total = bands * fields
    pairs, _, half = legendre.shape
    wave_ids = lax.iota(jnp.int32, waves)
    wave_count = jnp.minimum(waves, row_length // 2)
    in_range = (wave_ids[None, :] < wave_count[:, None])[None, :, None, :]
    nothing = jnp.zeros((), jnp.bfloat16)
    masked = jnp.where(in_range, fourier, nothing)
    start_pair = (band * fields + lax.axis_index("field")) * pairs
    pair_first = lax.dynamic_slice_in_dim(wave_order, start_pair, pairs)
    width = 2 * levels * lats

    if (bands, fields, lats, half, waves, pairs, levels) == (8, 4, 32, 128, 1024, 16, 36):
        spare, edge = half // 4, waves // 2
        turned = band >= bands // 2
        in_band = (band == 1) | (band == bands - 2)
        spare_lat = jnp.where(turned, lats - 1, 0)
        shared_lat = jnp.where(turned, 0, lats - 1)
        lat_ids = lax.iota(jnp.int32, lats)[None, :, None, None]
        wave_at = wave_ids[None, None, None, :]
        to_spare = in_band & (lat_ids == spare_lat) & (wave_at >= edge - 8) & (wave_at < edge)
        to_shared = in_band & (lat_ids == shared_lat) & (wave_at >= edge) & (wave_at < edge + 8)
        row = lax.dynamic_slice_in_dim(fourier, shared_lat, 1, axis=1)[..., edge : edge + 8]
        count = lax.dynamic_slice_in_dim(wave_count, shared_lat, 1, axis=0)
        row = jnp.where(wave_ids[edge : edge + 8] < count[0], row, nothing)
        pad = ((0, 0), (0, 0), (0, 0), (edge - 8, waves - edge))
        masked = jnp.where(to_spare, jnp.pad(jnp.flip(row, 3), pad), masked)

        by_holder = wave_order.reshape(total, pairs)
        ordering = jnp.concatenate([by_holder, waves - 1 - by_holder], axis=1).reshape(waves)
        choose = (ordering[:, None] == wave_ids[None, :]).astype(jnp.bfloat16)
        outgoing = spread_waves(choose, masked).reshape(bands, fields, 2, pairs, width)
        mixing = mixing_by_rows(vertical, fields, 128 // lats)
        back = packed_transform(
            outward(outgoing), legendre, mixing, pair_first, waves, lats, spare
        )
        restored = gather_waves(homeward(back).reshape(waves, width), choose, fourier.shape)
        row = lax.dynamic_slice_in_dim(restored, spare_lat, 1, axis=1)[..., edge - 8 : edge]
        pad = ((0, 0), (0, 0), (0, 0), (edge, waves - edge - 8))
        restored = jnp.where(to_shared, jnp.pad(jnp.flip(row, 3), pad), restored)
        return jnp.where(in_range, restored, nothing)

    ordering = jnp.stack([wave_order, waves - 1 - wave_order], axis=1).reshape(waves)
    choose = (ordering[:, None] == wave_ids[None, :]).astype(jnp.bfloat16)
    outgoing = spread_waves(choose, masked)
    arrived = exchange(outgoing.reshape(total, 2 * pairs, width), bands, fields, 2)
    values = arrived.reshape(bands, fields, pairs, 2, 2 * levels, lats).transpose(2, 1, 4, 3, 0, 5)
    values = values.reshape(pairs, fields * 2 * levels, 2 * bands * lats)
    grid_part = transform(values, legendre, mixing_matrix(vertical, fields), pair_first, waves)
    back = grid_part.reshape(pairs, fields, 2 * levels, 2, bands, lats).transpose(4, 1, 0, 3, 2, 5)
    home = exchange(back.reshape(total, 2 * pairs, width), bands, fields, 3)
    return jnp.where(in_range, gather_waves(home.reshape(waves, width), choose, fourier.shape), nothing)


def solution(mesh):
    placed = (P("field", "band", None, None), P("band"), P(), P(("band", "field"), None, None), P())
    return jax.shard_map(
        per_device,
        mesh=mesh,
        in_specs=placed,
        out_specs=P("field", "band", None, None),
        check_vma=False,
    )
```

```python
import functools

import jax
import jax.numpy as jnp
import numpy as np
from jax import lax
from jax.experimental import pallas as pl
from jax.experimental.pallas import tpu as pltpu
from jax.sharding import PartitionSpec as P

MESH = pl.DeviceIdType.MESH


def exchange_kernel(bands, fields, src, dst, send_sem, recv_sem, own_sem):
    total = bands * fields
    band, field = lax.axis_index("band"), lax.axis_index("field")
    me = band * fields + field

    def other(step):
        peer = lax.rem(me + step, total)
        return peer, (peer // fields, lax.rem(peer, fields))

    barrier = pltpu.get_barrier_semaphore()

    @pl.loop(1, total)
    def _(step):
        _, where = other(step)
        pl.semaphore_signal(barrier, inc=1, device_id=where, device_id_type=MESH)

    own = pltpu.make_async_copy(src.at[me], dst.at[me], own_sem)
    own.start()
    pl.semaphore_wait(barrier, total - 1)

    def copy(step):
        peer, where = other(step)
        return pltpu.make_async_remote_copy(
            src_ref=src.at[peer],
            dst_ref=dst.at[me],
            send_sem=send_sem.at[step],
            recv_sem=recv_sem.at[step],
            device_id=where,
            device_id_type=MESH,
        )

    @pl.loop(1, total)
    def _(step):
        copy(step).start()

    @pl.loop(1, total)
    def _(step):
        copy(step).wait_send()
        peer = lax.rem(me + total - step, total)
        pltpu.make_async_remote_copy(
            src_ref=src.at[peer],
            dst_ref=dst.at[peer],
            send_sem=send_sem.at[step],
            recv_sem=recv_sem.at[step],
            device_id=(peer // fields, lax.rem(peer, fields)),
            device_id_type=MESH,
        ).wait_recv()

    own.wait()


def exchange(data, bands, fields, ident):
    total = bands * fields
    return pl.pallas_call(
        functools.partial(exchange_kernel, bands, fields),
        out_shape=jax.ShapeDtypeStruct(data.shape, data.dtype),
        in_specs=[pl.BlockSpec(memory_space=pl.ANY)],
        out_specs=pl.BlockSpec(memory_space=pl.ANY),
        scratch_shapes=[
            pltpu.SemaphoreType.DMA((total,)),
            pltpu.SemaphoreType.DMA((total,)),
            pltpu.SemaphoreType.DMA,
        ],
        compiler_params=pltpu.CompilerParams(collective_id=ident, has_side_effects=True),
    )(data)


def pair_kernel(waves, first, x_ref, table_ref, mix_ref, out_ref):
    full = masked_table(waves, first[pl.program_id(0)], table_ref[0])
    out_ref[0] = there_and_back(x_ref[0], full, mix_ref[...]).astype(jnp.bfloat16)


def transform(values, legendre, mixing, pair_first, waves):
    pairs, columns, span = values.shape
    rows, half = legendre.shape[1:]
    flops = 2 * pairs * columns * rows * (2 * span + columns)
    return pl.pallas_call(
        functools.partial(pair_kernel, waves),
        grid_spec=pltpu.PrefetchScalarGridSpec(
            num_scalar_prefetch=1,
            grid=(pairs,),
            in_specs=[
                pl.BlockSpec((1, columns, span), lambda k, first: (k, 0, 0)),
                pl.BlockSpec((1, rows, half), lambda k, first: (k, 0, 0)),
                pl.BlockSpec((columns, columns), lambda k, first: (0, 0)),
            ],
            out_specs=pl.BlockSpec((1, columns, span), lambda k, first: (k, 0, 0)),
        ),
        out_shape=jax.ShapeDtypeStruct(values.shape, jnp.bfloat16),
        compiler_params=pltpu.CompilerParams(vmem_limit_bytes=48 * 1024 * 1024),
        cost_estimate=pl.CostEstimate(
            flops=flops, bytes_accessed=4 * values.size + 2 * legendre.size, transcendentals=0
        ),
    )(pair_first, values, legendre, mixing)


def swap_groups(parts, lats):
    lane_group = lax.broadcasted_iota(jnp.int32, parts[0].shape, 1) // lats
    swapped = []
    for j in range(len(parts)):
        merged = None
        for i, part in enumerate(parts):
            shift = ((i - j) * lats) % 128
            turned = pltpu.roll(part, shift, 1) if shift else part
            merged = turned if merged is None else jnp.where(lane_group == i, turned, merged)
        swapped.append(merged)
    return swapped


def masked_table(waves, first_wave, table):
    rows, half = table.shape
    boundary = waves - first_wave
    up = lax.broadcasted_iota(jnp.int32, (half, half), 0)
    across = lax.broadcasted_iota(jnp.int32, (half, half), 1)
    turn = (up + across == half - 1).astype(jnp.float32).astype(jnp.bfloat16)
    southern = jnp.dot(table, turn, preferred_element_type=jnp.float32)
    northern = table.astype(jnp.float32)
    row_ids = lax.broadcasted_iota(jnp.int32, (rows, half), 0)
    held = row_ids < boundary
    degree = jnp.where(held, row_ids, row_ids - boundary)
    southern = jnp.where(degree % 2 == 0, southern, -southern)
    zero = jnp.zeros((), jnp.float32)
    return jnp.concatenate(
        [
            jnp.where(held, northern, zero).astype(jnp.bfloat16),
            jnp.where(held, southern, zero).astype(jnp.bfloat16),
            jnp.where(held, zero, northern).astype(jnp.bfloat16),
            jnp.where(held, zero, southern).astype(jnp.bfloat16),
        ],
        axis=1,
    )


def there_and_back(values, full, mixing):
    spectral = lax.dot_general(
        values, full, (((1,), (1,)), ((), ())), preferred_element_type=jnp.float32
    ).astype(jnp.bfloat16)
    updated = jnp.dot(mixing, spectral, preferred_element_type=jnp.float32).astype(jnp.bfloat16)
    return jnp.dot(updated, full, preferred_element_type=jnp.float32)


ROUNDS = (2, 3, 1, 0)


def partner(field, turn):
    if turn == 0:
        return field
    if turn == 2:
        return lax.rem(field + 2, 4)
    return 3 - field if turn == 3 else field + 1 - 2 * lax.rem(field, 2)


def near_equator(band, bands):
    return (band >= bands // 4) & (band < bands - bands // 4)


def greet(band, field, bands):
    barrier = pltpu.get_barrier_semaphore()

    @pl.loop(1, bands)
    def _(step):
        where = (lax.rem(band + step, bands), field)
        pl.semaphore_signal(barrier, inc=1, device_id=where, device_id_type=MESH)

    for turn in (1, 2, 3):
        where = (band, partner(field, turn))
        pl.semaphore_signal(barrier, inc=1, device_id=where, device_id_type=MESH)
    pl.semaphore_wait(barrier, bands - 1 + 3)


def remote(src, dst, send, recv, where):
    return pltpu.make_async_remote_copy(
        src_ref=src, dst_ref=dst, send_sem=send, recv_sem=recv, device_id=where, device_id_type=MESH
    )


def outward_kernel(bands, src, dst, mid, plane_send, plane_recv, line_send, line_recv, own_sem, last_sem):
    band, field = lax.axis_index("band"), lax.axis_index("field")
    middle = pl.ds(bands // 2 - 1, 2)
    greet(band, field, bands)

    def plane(turn, step, slot):
        peer = lax.rem(band + step, bands)
        return remote(
            src.at[peer, partner(field, turn), slot], mid.at[turn, slot, band],
            plane_send.at[turn, step, slot], plane_recv.at[turn, step, slot], (peer, field),
        )

    def arrival(turn, step, slot):
        peer = lax.rem(band + bands - step, bands)
        spot = mid.at[turn, slot, peer]
        return remote(
            spot, spot, plane_send.at[turn, step, slot], plane_recv.at[turn, step, slot], (peer, field)
        )

    def own(turn, slot):
        return pltpu.make_async_copy(
            src.at[band, partner(field, turn), slot], mid.at[turn, slot, band], own_sem.at[turn, slot]
        )

    def ends(turn, slot, origin):
        if slot == 0:
            return mid.at[turn, 0], dst.at[origin, 0]
        return mid.at[turn, 1, middle], dst.at[origin, 1, middle]

    def line(turn, slot):
        source, target = ends(turn, slot, field)
        where = (band, partner(field, turn))
        return remote(source, target, line_send.at[turn, slot], line_recv.at[turn, slot], where)

    def line_arrival(turn, slot):
        origin = partner(field, turn)
        spot = ends(turn, slot, origin)[1]
        return remote(
            spot, spot, line_send.at[turn, slot], line_recv.at[turn, slot], (band, origin)
        )

    def last(slot):
        source, target = ends(0, slot, field)
        return pltpu.make_async_copy(source, target, last_sem.at[slot])

    def begin(turn):
        own(turn, 0).start()
        own(turn, 1).start()

        @pl.loop(1, bands)
        def _(step):
            plane(turn, step, 0).start()

            @pl.when(near_equator(band, bands))
            def _():
                plane(turn, step, 1).start()

    begin(ROUNDS[0])
    for at, turn in enumerate(ROUNDS):
        own(turn, 0).wait()
        own(turn, 1).wait()

        @pl.loop(1, bands)
        def _(step):
            arrival(turn, step, 0).wait_recv()

            @pl.when(near_equator(lax.rem(band + bands - step, bands), bands))
            def _():
                arrival(turn, step, 1).wait_recv()

        if at + 1 < len(ROUNDS):
            begin(ROUNDS[at + 1])
        for pole, mate in ((0, bands - bands // 4 - 1), (bands - 1, bands // 4)):
            mid[turn, 0, pole] = mid[turn, 0, pole] + mid[turn, 1, mate]
        for slot in range(2):
            if turn:
                line(turn, slot).start()
            else:
                last(slot).start()

    for turn in ROUNDS:

        @pl.loop(1, bands)
        def _(step):
            plane(turn, step, 0).wait_send()

            @pl.when(near_equator(band, bands))
            def _():
                plane(turn, step, 1).wait_send()

        for slot in range(2):
            if turn:
                line(turn, slot).wait_send()
                line_arrival(turn, slot).wait_recv()
            else:
                last(slot).wait()


def homeward_kernel(
    bands, src, zeros, dst, mid, plane_send, plane_recv, line_send, line_recv, own_sem, zero_sem
):
    band, field = lax.axis_index("band"), lax.axis_index("field")
    middle = pl.ds(bands // 2 - 1, 2)
    greet(band, field, bands)

    def held(turn, slot, target):
        return src.at[field, slot, target] if turn == 0 else mid.at[turn, slot, target]

    def second_slot(turn, target, act):
        north, south = bands // 4, bands - bands // 4 - 1

        @pl.when(target == north)
        def _():
            act(held(turn, 0, bands - 1))

        @pl.when(target == south)
        def _():
            act(held(turn, 0, 0))

        @pl.when((target > north) & (target < south))
        def _():
            act(held(turn, 1, target))

    def plane(turn, step, slot, source):
        peer = lax.rem(band + step, bands)
        return remote(
            source, dst.at[band, partner(field, turn), slot],
            plane_send.at[turn, step, slot], plane_recv.at[turn, step, slot], (peer, field),
        )

    def arrival(turn, step, slot):
        peer = lax.rem(band + bands - step, bands)
        spot = dst.at[peer, partner(field, turn), slot]
        return remote(
            spot, spot, plane_send.at[turn, step, slot], plane_recv.at[turn, step, slot], (peer, field)
        )

    def own(turn, slot, source):
        return pltpu.make_async_copy(
            source, dst.at[band, partner(field, turn), slot], own_sem.at[turn, slot]
        )

    def blank(peer, z):
        return pltpu.make_async_copy(zeros, dst.at[peer, z, 1], zero_sem.at[peer, z])

    def line(turn, slot):
        goal = partner(field, turn)
        if slot == 0:
            source, target = src.at[goal, 0], mid.at[turn, 0]
        else:
            source, target = src.at[goal, 1, middle], mid.at[turn, 1, middle]
        return remote(
            source, target, line_send.at[turn, slot], line_recv.at[turn, slot], (band, goal)
        )

    def spread(turn):
        @pl.loop(1, bands)
        def _(step):
            peer = lax.rem(band + step, bands)
            plane(turn, step, 0, held(turn, 0, peer)).start()
            second_slot(turn, peer, lambda source: plane(turn, step, 1, source).start())

        own(turn, 0, held(turn, 0, band)).start()
        second_slot(turn, band, lambda source: own(turn, 1, source).start())

    for turn in (2, 1):
        line(turn, 0).start()
        line(turn, 1).start()
    spread(0)

    @pl.when(jnp.logical_not(near_equator(band, bands)))
    def _():
        @pl.loop(0, bands)
        def _(peer):
            for z in range(4):
                blank(peer, z).start()

    for slot in range(2):
        line(2, slot).wait_recv()
        line(3, slot).start()
    spread(2)
    for turn in (1, 3):
        line(turn, 0).wait_recv()
        line(turn, 1).wait_recv()
        spread(turn)

    @pl.when(jnp.logical_not(near_equator(band, bands)))
    def _():
        @pl.loop(0, bands)
        def _(peer):
            for z in range(4):
                blank(peer, z).wait()

    for turn in (0, 2, 1, 3):
        own(turn, 0, held(turn, 0, band)).wait()

        @pl.when(near_equator(band, bands))
        def _():
            own(turn, 1, held(turn, 1, band)).wait()

        @pl.loop(1, bands)
        def _(step):
            peer = lax.rem(band + step, bands)
            plane(turn, step, 0, held(turn, 0, peer)).wait_send()
            arrival(turn, step, 0).wait_recv()
            second_slot(turn, peer, lambda source: plane(turn, step, 1, source).wait_send())

            @pl.when(near_equator(band, bands))
            def _():
                arrival(turn, step, 1).wait_recv()

        if turn:
            line(turn, 0).wait_send()
            line(turn, 1).wait_send()


def staged_scratch(bands, piece):
    return [
        pltpu.VMEM((4, 2, bands) + piece, jnp.bfloat16),
        pltpu.SemaphoreType.DMA((4, bands, 2)),
        pltpu.SemaphoreType.DMA((4, bands, 2)),
        pltpu.SemaphoreType.DMA((4, 2)),
        pltpu.SemaphoreType.DMA((4, 2)),
        pltpu.SemaphoreType.DMA((4, 2)),
    ]


def outward(data):
    bands, fields, _, count, width = data.shape
    return pl.pallas_call(
        functools.partial(outward_kernel, bands),
        out_shape=jax.ShapeDtypeStruct((fields, 2, bands, count, width), data.dtype),
        in_specs=[pl.BlockSpec(memory_space=pl.ANY)],
        out_specs=pl.BlockSpec(memory_space=pl.ANY),
        scratch_shapes=staged_scratch(bands, (count, width)) + [pltpu.SemaphoreType.DMA((2,))],
        compiler_params=pltpu.CompilerParams(
            collective_id=0, has_side_effects=True, vmem_limit_bytes=12 * 1024 * 1024
        ),
    )(data)


def homeward(data):
    fields, _, bands, count, width = data.shape
    return pl.pallas_call(
        functools.partial(homeward_kernel, bands),
        out_shape=jax.ShapeDtypeStruct((bands, fields, 2, count, width), data.dtype),
        in_specs=[pl.BlockSpec(memory_space=pl.ANY)] * 2,
        out_specs=pl.BlockSpec(memory_space=pl.ANY),
        scratch_shapes=staged_scratch(bands, (count, width)) + [pltpu.SemaphoreType.DMA((bands, 4))],
        compiler_params=pltpu.CompilerParams(
            collective_id=1, has_side_effects=True, vmem_limit_bytes=12 * 1024 * 1024
        ),
    )(data, jnp.zeros((count, width), data.dtype))


def lane_origins(half):
    lane = np.arange(half)
    columns = [
        half - 1 - lane,
        np.where(lane < half // 2, lane + half // 2, half + half // 2 - 1 - lane),
        half - half // 4 - 1 - lane,
        lane - half // 4,
    ]
    return (np.arange(half)[:, None] == np.concatenate(columns)[None, :]).astype(np.float32)


def compact_table(waves, first_wave, table, select, spare):
    rows, half = table.shape
    boundary = waves - first_wave
    row_ids = lax.broadcasted_iota(jnp.int32, (rows, half), 0)
    lanes = lax.broadcasted_iota(jnp.int32, (1, half), 1)
    held = row_ids < boundary
    degree = jnp.where(held, row_ids, row_ids - boundary)
    sign = (1 - 2 * (degree % 2)).astype(jnp.float32)
    variants = jnp.dot(table.astype(jnp.bfloat16), select, preferred_element_type=jnp.float32)
    turned, extra, mirrored, mirrored_south = [
        variants[:, i * half : (i + 1) * half] for i in range(4)
    ]

    def shares(from_pole):
        mates = (from_pole < half // 4) & (first_wave >= half // 8 + waves // half * from_pole)
        moved = (from_pole == spare) & (first_wave >= waves // 2 - 8)
        mates, moved = mates.astype(jnp.float32), moved.astype(jnp.float32)
        return mates, moved, 1.0 - mates - moved

    mates, moved, kept = shares(lanes)
    main = jnp.where(held, table * kept, mirrored * (sign * mates + moved))
    mates, moved, kept = shares(half - 1 - lanes)
    southern = jnp.where(held, turned * (sign * kept), mirrored_south * (mates + sign * moved))
    upper = (lanes < half // 2).astype(jnp.float32)
    extra = jnp.where(held, 0.0, extra * (upper + sign * (1.0 - upper)))
    return jnp.concatenate([main, southern, extra], axis=1).astype(jnp.bfloat16)


def packed_kernel(
    waves, lats, spare, first, x_ref, table_ref, mix_ref, select_ref, out_ref, held_ref, wide_ref
):
    k = pl.program_id(0)
    fields, _, bands, count, width = x_ref.shape
    tiles = width // 128
    group = 128 // lats
    rows = fields * tiles
    low, high = bands // 4, bands - bands // 4
    spans = [(0, 0, bands, 0), (1, low + 1, high - 1, bands + 1)]

    @pl.when(k == 0)
    def _():
        row_total, pairs, half = table_ref.shape
        step = next(n for n in range(32, 0, -1) if row_total % n == 0)

        @pl.loop(0, row_total // step)
        def _(i):
            block = table_ref[pl.ds(i * step, step)].astype(jnp.float32)
            for n in range(step):
                wide_ref[pl.ds((i * step + n) * (pairs + 1), pairs), :] = block[n]

        held_ref[bands] = jnp.zeros(held_ref.shape[1:], jnp.float32)
        held_ref[bands + high - low - 1] = jnp.zeros(held_ref.shape[1:], jnp.float32)
        for slot, begin, end, base in spans:

            @pl.loop(begin, end)
            def _(band):
                for field in range(fields):
                    for tile in range(tiles):
                        at = (field * tiles + tile) * (count + 1)
                        held_ref[base - begin + band, at : at + count, :] = x_ref[
                            field, slot, band, :, tile * 128 : (tile + 1) * 128
                        ].astype(jnp.float32)

    place = pl.ds(k, rows, stride=count + 1)
    slabs = bands + high - low
    gathered = [[] for _ in range(group)]
    for start in range(0, slabs, group):
        parts = [held_ref[start + i, place, :] for i in range(group)]
        for j, part in enumerate(swap_groups(parts, lats)):
            gathered[j].append(part)
    values = jnp.concatenate([jnp.concatenate(g, axis=1) for g in gathered], axis=0).astype(jnp.bfloat16)
    table = wide_ref[pl.ds(k, table_ref.shape[0], stride=table_ref.shape[1] + 1), :]
    full = compact_table(waves, first[k], table, select_ref[...], spare)
    result = there_and_back(values, full, mix_ref[...])
    for start in range(0, slabs, group):
        at = start * lats
        parts = [result[j * rows : (j + 1) * rows, at : at + 128] for j in range(group)]
        for i, part in enumerate(swap_groups(parts, lats)):
            held_ref[start + i, place, :] = part

    @pl.when(k == pl.num_programs(0) - 1)
    def _():
        for slot, begin, end, base in spans:

            @pl.loop(begin, end)
            def _(band):
                for field in range(fields):
                    for tile in range(tiles):
                        at = (field * tiles + tile) * (count + 1)
                        out_ref[field, slot, band, :, tile * 128 : (tile + 1) * 128] = held_ref[
                            base - begin + band, at : at + count, :
                        ].astype(jnp.bfloat16)


def packed_transform(arrived, legendre, mixing, pair_first, waves, lats, spare):
    fields, _, bands, count, width = arrived.shape
    pairs, rows, half = legendre.shape
    columns = mixing.shape[0]
    flops = 2 * pairs * columns * rows * (3 * bands * lats + columns)
    whole = pl.BlockSpec(arrived.shape, lambda k, first: (0, 0, 0, 0, 0))
    slabs = bands + bands - 2 * (bands // 4)
    select = jnp.asarray(lane_origins(half), jnp.bfloat16)
    return pl.pallas_call(
        functools.partial(packed_kernel, waves, lats, spare),
        grid_spec=pltpu.PrefetchScalarGridSpec(
            num_scalar_prefetch=1,
            grid=(pairs,),
            in_specs=[
                whole,
                pl.BlockSpec((rows, pairs, half), lambda k, first: (0, 0, 0)),
                pl.BlockSpec((columns, columns), lambda k, first: (0, 0)),
                pl.BlockSpec(select.shape, lambda k, first: (0, 0)),
            ],
            out_specs=whole,
            scratch_shapes=[
                pltpu.VMEM((slabs, fields * width // 128 * (count + 1), 128), jnp.float32),
                pltpu.VMEM((-(-rows * (pairs + 1) // 8) * 8, half), jnp.float32),
            ],
        ),
        out_shape=jax.ShapeDtypeStruct(arrived.shape, jnp.bfloat16),
        compiler_params=pltpu.CompilerParams(vmem_limit_bytes=56 * 1024 * 1024),
        cost_estimate=pl.CostEstimate(
            flops=flops, bytes_accessed=4 * arrived.size + 2 * legendre.size, transcendentals=0
        ),
    )(pair_first, arrived, legendre.transpose(1, 0, 2), mixing, select)


def mixing_by_rows(vertical, fields, group):
    levels = vertical.shape[1]
    per_field = 2 * levels // fields
    tiles = 2 * per_field // group
    j, z, t = np.meshgrid(np.arange(group), np.arange(fields), np.arange(tiles), indexing="ij")
    column = (t * group + j).reshape(-1)
    part = column // per_field
    level = z.reshape(-1) * per_field + column % per_field
    rows = level.size
    choose = np.zeros((2, rows, levels), np.float32)
    choose[level // levels, np.arange(rows), level % levels] = 1
    choose = jnp.asarray(choose, jnp.bfloat16)
    left = jnp.einsum("qra,qab->rqb", choose, vertical, preferred_element_type=jnp.float32)
    both = jnp.einsum(
        "rqb,qsb->rs", left.astype(jnp.bfloat16), choose, preferred_element_type=jnp.float32
    )
    return jnp.where(jnp.asarray(part[:, None] == part[None, :]), both, 0.0).astype(jnp.bfloat16)


def mixing_matrix(vertical, fields):
    levels = vertical.shape[1]
    total = 2 * levels
    blocks = jnp.zeros((2, levels, 2, levels), vertical.dtype)
    blocks = blocks.at[0, :, 0, :].set(vertical[0]).at[1, :, 1, :].set(vertical[1])
    block = blocks.reshape(fields, total // fields, fields, total // fields)
    parts = jnp.eye(2, dtype=vertical.dtype)
    return jnp.einsum("zfyg,cd->zcfydg", block, parts).reshape(2 * total, 2 * total)


def spread_waves(choose, masked):
    levels, lats, _, waves = masked.shape
    flat = masked.transpose(2, 0, 1, 3).reshape(2 * levels * lats, waves)
    return lax.dot_general(
        choose, flat, (((1,), (1,)), ((), ())), preferred_element_type=jnp.float32
    ).astype(jnp.bfloat16)


def gather_waves(home, choose, shape):
    levels, lats, _, waves = shape
    restored = lax.dot_general(
        home, choose, (((0,), (0,)), ((), ())), preferred_element_type=jnp.float32
    ).astype(jnp.bfloat16)
    return restored.reshape(2, levels, lats, waves).transpose(1, 2, 0, 3)


def per_device(fourier, row_length, wave_order, legendre, vertical):
    levels, lats, _, waves = fourier.shape
    bands, fields = lax.axis_size("band"), lax.axis_size("field")
    band = lax.axis_index("band")
    total = bands * fields
    pairs, _, half = legendre.shape
    wave_ids = lax.iota(jnp.int32, waves)
    wave_count = jnp.minimum(waves, row_length // 2)
    in_range = (wave_ids[None, :] < wave_count[:, None])[None, :, None, :]
    nothing = jnp.zeros((), jnp.bfloat16)
    masked = jnp.where(in_range, fourier, nothing)
    start_pair = (band * fields + lax.axis_index("field")) * pairs
    pair_first = lax.dynamic_slice_in_dim(wave_order, start_pair, pairs)
    width = 2 * levels * lats

    if (bands, fields, lats, half, waves, pairs, levels) == (8, 4, 32, 128, 1024, 16, 36):
        spare, edge = half // 4, waves // 2
        turned = band >= bands // 2
        in_band = (band == 1) | (band == bands - 2)
        spare_lat = jnp.where(turned, lats - 1, 0)
        shared_lat = jnp.where(turned, 0, lats - 1)
        lat_ids = lax.iota(jnp.int32, lats)[None, :, None, None]
        wave_at = wave_ids[None, None, None, :]
        to_spare = in_band & (lat_ids == spare_lat) & (wave_at >= edge - 8) & (wave_at < edge)
        to_shared = in_band & (lat_ids == shared_lat) & (wave_at >= edge) & (wave_at < edge + 8)
        row = lax.dynamic_slice_in_dim(fourier, shared_lat, 1, axis=1)[..., edge : edge + 8]
        count = lax.dynamic_slice_in_dim(wave_count, shared_lat, 1, axis=0)
        row = jnp.where(wave_ids[edge : edge + 8] < count[0], row, nothing)
        pad = ((0, 0), (0, 0), (0, 0), (edge - 8, waves - edge))
        masked = jnp.where(to_spare, jnp.pad(jnp.flip(row, 3), pad), masked)

        by_holder = wave_order.reshape(total, pairs)
        ordering = jnp.concatenate([by_holder, waves - 1 - by_holder], axis=1).reshape(waves)
        choose = (ordering[:, None] == wave_ids[None, :]).astype(jnp.bfloat16)
        outgoing = spread_waves(choose, masked).reshape(bands, fields, 2, pairs, width)
        mixing = mixing_by_rows(vertical, fields, 128 // lats)
        back = packed_transform(
            outward(outgoing), legendre, mixing, pair_first, waves, lats, spare
        )
        restored = gather_waves(homeward(back).reshape(waves, width), choose, fourier.shape)
        row = lax.dynamic_slice_in_dim(restored, spare_lat, 1, axis=1)[..., edge - 8 : edge]
        pad = ((0, 0), (0, 0), (0, 0), (edge, waves - edge - 8))
        restored = jnp.where(to_shared, jnp.pad(jnp.flip(row, 3), pad), restored)
        return jnp.where(in_range, restored, nothing)

    ordering = jnp.stack([wave_order, waves - 1 - wave_order], axis=1).reshape(waves)
    choose = (ordering[:, None] == wave_ids[None, :]).astype(jnp.bfloat16)
    outgoing = spread_waves(choose, masked)
    arrived = exchange(outgoing.reshape(total, 2 * pairs, width), bands, fields, 2)
    values = arrived.reshape(bands, fields, pairs, 2, 2 * levels, lats).transpose(2, 1, 4, 3, 0, 5)
    values = values.reshape(pairs, fields * 2 * levels, 2 * bands * lats)
    grid_part = transform(values, legendre, mixing_matrix(vertical, fields), pair_first, waves)
    back = grid_part.reshape(pairs, fields, 2 * levels, 2, bands, lats).transpose(4, 1, 0, 3, 2, 5)
    home = exchange(back.reshape(total, 2 * pairs, width), bands, fields, 3)
    return jnp.where(in_range, gather_waves(home.reshape(waves, width), choose, fourier.shape), nothing)


def solution(mesh):
    placed = (P("field", "band", None, None), P("band"), P(), P(("band", "field"), None, None), P())
    return jax.shard_map(
        per_device,
        mesh=mesh,
        in_specs=placed,
        out_specs=P("field", "band", None, None),
        check_vma=False,
    )
```
